32 devices in a mesh: img: 16 (over z, y, x), pix: 2 (over core).
Axes of the slice: x: 2, y: 2, z: 4, core: 2. Of those that a mesh axis runs over, the one named last changes fastest.
Arguments:
- images: bfloat16 [4096, 16384], P('img', 'pix'), may hold values from -100 to 100
- references: bfloat16 [1536, 16384], P('img', 'pix'), may hold values from -6 to 6
- cycle_mask: int32 [16384], P('pix'), may hold values from 0 to 1, as said below
- view_class: int32 [1536], replicated, may hold values from 0 to 95, as said below
Outputs:
- view_sums: float32 [1536, 16384], P('img', 'pix')
- class_share: float32 [96], replicated
- image_evidence: float32 [4096], P(('img', 'pix'))
The draws below stay inside these ranges and needn't reach their ends.
Inputs may be any that keep to these rules, and one draw needn't show every extreme that they name: `cycle_mask`: only pixels whose distance from the image centre lies between an inner radius and 64 are 1; some of them are left out as defective, never those in even columns, so the cycle is never empty. `view_class`: every class is named by exactly 16 views.
All inputs are finite; a program needn't handle non-finite values.
Results may differ from the reference program's by a relative error of at most 0.0023.
Values may be sent and summed in bfloat16 or wider, within the bound.
A program may use at most 128 MiB of HBM per device.

```python
import math
import jax
import jax.numpy as jnp
from jax import lax

SIDE = 128
NCLS = 96
ROT = 16
IMG_DEV = 256
NIMG = 4096
PIX = 16384
NREF = 1536


def template_views(key):
    base_key = jax.random.fold_in(key, 101)
    return jax.random.truncated_normal(base_key, -5.0, 5.0, (NREF, PIX), jnp.float32)


def draw_references(key, part):
    return template_views(key).astype(jnp.bfloat16)


def draw_images(key, part):
    views = template_views(key)
    pix_mean = jax.random.truncated_normal(jax.random.fold_in(key, 201), -3.0, 3.0, (PIX,), jnp.float32)
    pix_scale = jnp.exp(jax.random.uniform(jax.random.fold_in(key, 202), (PIX,), jnp.float32, 0.0, math.log(4.0)))
    chosen = 2 * jax.random.randint(jax.random.fold_in(key, 203), (NIMG,), 0, NREF // 2)
    signal = views[chosen]
    level = 0.005 + 0.02 * jnp.arange(NIMG, dtype=jnp.float32) / NIMG
    noise = jax.random.truncated_normal(jax.random.fold_in(key, 204), -5.0, 5.0, (NIMG, PIX), jnp.float32)
    img_scale = jnp.exp(jax.random.uniform(jax.random.fold_in(key, 205), (NIMG, 1), jnp.float32, math.log(0.5), math.log(2.0)))
    img_shift = 0.5 * jax.random.truncated_normal(jax.random.fold_in(key, 206), -4.0, 4.0, (NIMG, 1), jnp.float32)
    clean = level[:, None] * signal + noise
    return (img_shift + img_scale * (pix_mean[None, :] + pix_scale[None, :] * clean)).astype(jnp.bfloat16)


def draw_cycle_mask(key, part):
    index = jnp.arange(PIX, dtype=jnp.int32)
    row_pos = index // SIDE
    col_pos = index % SIDE
    distance = (2 * row_pos + 1 - SIDE) ** 2 + (2 * col_pos + 1 - SIDE) ** 2
    inner = jax.random.randint(jax.random.fold_in(key, 301), (), SIDE * 5 // 16, SIDE * 7 // 16 + 1)
    usable = jax.random.randint(jax.random.fold_in(key, 302), (PIX,), 0, 8)
    kept = (usable != 0) | (col_pos % 2 == 0)
    return ((distance >= (2 * inner) ** 2) & (distance < SIDE * SIDE) & kept).astype(jnp.int32)


def draw_view_class(key, part):
    order = jax.random.permutation(jax.random.fold_in(key, 401), NREF)
    return (order // ROT).astype(jnp.int32)


def setup_inputs(seed: int = 0) -> dict:
    arg_keys = jax.random.split(jax.random.key(seed), 5)
    images = draw_images(jax.random.fold_in(arg_keys[4], 71), 0)
    references = draw_references(jax.random.fold_in(arg_keys[4], 71), 0)
    cycle_mask = draw_cycle_mask(jax.random.fold_in(arg_keys[4], 71), 0)
    view_class = draw_view_class(jax.random.fold_in(arg_keys[4], 71), 0)
    return {"images": images, "references": references, "cycle_mask": cycle_mask, "view_class": view_class}


EPSILON = 1e-05

def reference(images, references, cycle_mask, view_class):
    total_images = images.shape[0]
    pixel_count = images.shape[1]
    blocks = images.reshape(total_images // IMG_DEV, IMG_DEV, pixel_count)

    def add_moments(carry, block):
        widened = block.astype(jnp.float32)
        return ((carry[0] + lax.optimization_barrier(jnp.sum(widened, 0)), carry[1] + lax.optimization_barrier(jnp.sum(widened * widened, 0))), None)
    zeros_pix = jnp.zeros((pixel_count,), jnp.float32)
    (col_sum, col_sq), _ = lax.scan(add_moments, (zeros_pix, zeros_pix), blocks)
    pix_mean = col_sum / total_images
    pix_std = jnp.sqrt(col_sq / total_images - pix_mean * pix_mean + EPSILON)
    cycle_weight = cycle_mask.astype(jnp.float32)
    cycle_count = jnp.sum(cycle_weight)
    ref_energy = lax.optimization_barrier(jnp.sum(jnp.square(references.astype(jnp.float32)), 1))
    onehot = (view_class[:, None] == jnp.arange(NCLS, dtype=jnp.int32)[None, :]).astype(jnp.float32)
    factor = 4.0 / SIDE

    def classify(carry, block):
        view_acc, class_acc = carry
        widened = block.astype(jnp.float32)
        whitened = (widened - pix_mean) / pix_std
        bg_mean = lax.optimization_barrier(jnp.sum(whitened * cycle_weight, 1)) / cycle_count
        bg_std = jnp.sqrt(lax.optimization_barrier(jnp.sum(whitened * whitened * cycle_weight, 1)) / cycle_count - bg_mean * bg_mean + EPSILON)
        normed = ((whitened - bg_mean[:, None]) / bg_std[:, None]).astype(jnp.bfloat16)
        raw = lax.dot_general(normed, references, (((1,), (1,)), ((), ())), preferred_element_type=jnp.float32)
        scores = (raw - 0.5 * ref_energy[None, :]) * factor
        row_max = lax.optimization_barrier(jnp.max(scores, 1, keepdims=True))
        log_total = row_max[:, 0] + jnp.log(lax.optimization_barrier(jnp.sum(jnp.exp(scores - row_max), 1)))
        evidence = log_total - lax.optimization_barrier(jnp.mean(scores, 1))
        posterior = jnp.exp(scores - log_total[:, None]).astype(jnp.bfloat16)
        view_acc = view_acc + lax.dot_general(posterior, normed, (((0,), (0,)), ((), ())), preferred_element_type=jnp.float32)
        class_mass = lax.optimization_barrier(jnp.sum(posterior, 0, dtype=jnp.float32))
        class_acc = class_acc + jnp.dot(class_mass, onehot, precision=lax.Precision.HIGHEST)
        return ((view_acc, class_acc), evidence)
    start_views = jnp.zeros((references.shape[0], pixel_count), jnp.float32)
    start_class = jnp.zeros((NCLS,), jnp.float32)
    (view_sums, class_total), evidence = lax.scan(classify, (start_views, start_class), blocks)
    return (view_sums, class_total * (NCLS / total_images), evidence.reshape(-1))
```

```python
import functools

import jax
import jax.numpy as jnp
from jax import lax
from jax.experimental import pallas as pl
from jax.experimental.pallas import tpu as pltpu
from jax.sharding import PartitionSpec as P

SIDE = 128
NCLS = 96
EPSILON = 1e-05
MESH = pl.DeviceIdType.MESH

PIXEL_BIT = 4
VIEW_BIT = 2


def image_bits(n):
    return [b for b in (1, *reversed([2**j for j in range(3, 20) if 2**j < n]))]


def bit(index, value):
    return (index // value) % 2


def flip(index, value):
    return index + value * (1 - 2 * bit(index, value))


def greet(partners):
    barrier = pltpu.get_barrier_semaphore()
    for p in partners:
        pl.semaphore_signal(barrier, inc=1, device_id={"img": p}, device_id_type=MESH)
    pl.semaphore_wait(barrier, len(partners))


def gather_kernel(n, chunks, images, refs, img_all, ref_all, lsem, isend, irecv, rsend, rrecv):
    d = lax.axis_index("img")
    bits = image_bits(n)
    nr = len(bits)
    k, c = bit(d, PIXEL_BIT), bit(d, VIEW_BIT)
    kp, cp = flip(d, PIXEL_BIT), flip(d, VIEW_BIT)
    rows, cols = images.shape
    q = cols // 2
    mine = pl.ds(pl.multiple_of(k * q, 128), q)
    theirs = pl.ds(pl.multiple_of((1 - k) * q, 128), q)
    weights = [2 ** (nr - j) for j in range(nr)]
    slot = k
    for b, w in zip(bits, weights):
        slot = slot + w * bit(d, b)

    greet([kp, cp] + [flip(d, b) for b in bits])

    def remote(src, dst, ssem, rsem, partner):
        cp_ = pltpu.make_async_remote_copy(
            src_ref=src, dst_ref=dst, send_sem=ssem, recv_sem=rsem,
            device_id={"img": partner}, device_id_type=MESH)
        cp_.start()
        return cp_

    step = rows // chunks
    own = 2 * c + k
    other = 2 * c + 1 - k
    ref_copies = []

    def send_ref(src, s, partner):
        i = len(ref_copies)
        ref_copies.append(remote(src, ref_all.at[s], rsend.at[i], rrecv.at[i], partner))
        return ref_copies[-1]

    img_copies = []

    def send_img(src, dst, partner):
        i = len(img_copies)
        img_copies.append(remote(src, dst, isend.at[i], irecv.at[i], partner))
        return img_copies[-1]

    order = list(reversed(list(zip(bits, weights))))
    pair_ref = send_ref(refs.at[:, theirs], slot, kp)
    own_refs = refs.at[:, mine]
    stage = [[] for _ in order]
    for j, (b, w) in enumerate(order):
        stage[j].append((send_ref(own_refs, slot, flip(d, b)), slot))
    img_k = []
    for i in range(chunks):
        r = pl.ds(i * step, step)
        img_k.append(send_img(images.at[r, theirs], img_all.at[own, r], kp))
    for i in range(chunks):
        r = pl.ds(i * step, step)
        send_img(images.at[r, mine], img_all.at[own, r], cp)
    local = [
        pltpu.make_async_copy(own_refs, ref_all.at[slot], lsem.at[0]),
        pltpu.make_async_copy(images.at[:, mine], img_all.at[own], lsem.at[1]),
    ]
    for x in local:
        x.start()

    waited = []

    def forward_img(i):
        r = pl.ds(i * step, step)
        img_k[i].wait_recv()
        waited.append(img_k[i])
        send_img(img_all.at[other, r], img_all.at[other, r], cp)

    def arrive(copy):
        copy.wait_recv()
        waited.append(copy)

    arrive(pair_ref)
    pair_slot = slot + 1 - 2 * k
    for j, (b, w) in enumerate(order):
        stage[j].append((send_ref(ref_all.at[pair_slot], pair_slot, flip(d, b)), pair_slot))
    done_img = 0
    for j, (b, w) in enumerate(order[:-1]):
        bj = bit(d, b)
        for copy, s in stage[j]:
            if done_img < chunks:
                forward_img(done_img)
                done_img += 1
            arrive(copy)
            got = s + w * (1 - 2 * bj)
            for j2 in range(j + 1, len(order)):
                stage[j2].append((send_ref(ref_all.at[got], got, flip(d, order[j2][0])), got))
    while done_img < chunks:
        forward_img(done_img)
        done_img += 1
    for copy in ref_copies + img_copies:
        if all(copy is not x for x in waited):
            copy.wait_recv()
    for copy in ref_copies + img_copies:
        copy.wait_send()
    for x in local:
        x.wait()


def gather(n, images, refs):
    rows, cols = images.shape
    chunks = 4
    n_ref = 1 + sum(2 ** (j + 1) for j in range(len(image_bits(n))))
    n_img = 3 * chunks
    hbm = pl.BlockSpec(memory_space=pl.ANY)
    return pl.pallas_call(
        functools.partial(gather_kernel, n, chunks),
        out_shape=(
            jax.ShapeDtypeStruct((4, rows, cols // 2), images.dtype),
            jax.ShapeDtypeStruct((n // 2, refs.shape[0], cols // 2), refs.dtype),
        ),
        in_specs=[hbm, hbm],
        out_specs=(hbm, hbm),
        scratch_shapes=[
            pltpu.SemaphoreType.DMA((2,)),
            pltpu.SemaphoreType.DMA((n_img,)),
            pltpu.SemaphoreType.DMA((n_img,)),
            pltpu.SemaphoreType.DMA((n_ref,)),
            pltpu.SemaphoreType.DMA((n_ref,)),
        ],
        compiler_params=pltpu.CompilerParams(
            collective_id=0, has_side_effects=True, vmem_limit_bytes=56 * 2**20),
    )(images, refs)


def sums_kernel(n, tiles, post, normed, out, *scratch):
    d = lax.axis_index("img")
    bits = image_bits(n)
    nr = len(bits)
    k, kp = bit(d, PIXEL_BIT), flip(d, PIXEL_BIT)
    q = normed.shape[1]
    w = q // tiles
    partners = [flip(d, b) for b in bits]
    mybits = [bit(d, b) for b in bits]
    keep = scratch[0]
    sends = scratch[1:1 + nr]
    recvs = scratch[1 + nr:1 + 2 * nr]
    last, ssem, rsem = scratch[1 + 2 * nr:]
    half0 = post.shape[1]

    greet([kp] + partners)

    def cols(t):
        return pl.ds(pl.multiple_of(t * w, 128), w)

    def stage_copy(j, t):
        return pltpu.make_async_remote_copy(
            src_ref=sends[j].at[t], dst_ref=recvs[j].at[t],
            send_sem=ssem.at[j, t], recv_sem=rsem.at[j, t],
            device_id={"img": partners[j]}, device_id_type=MESH)

    def last_copy(t):
        place = pl.ds(pl.multiple_of(k * q + t * w, 128), w)
        return pltpu.make_async_remote_copy(
            src_ref=last.at[t], dst_ref=out.at[:, place],
            send_sem=ssem.at[nr, t], recv_sem=rsem.at[nr, t],
            device_id={"img": kp}, device_id_type=MESH)

    def first(t, _):
        sends[0][t] = jnp.dot(
            post[1 - mybits[0]], normed[:, cols(t)], preferred_element_type=jnp.float32
        ).astype(jnp.bfloat16)
        stage_copy(0, t).start()
        return 0

    lax.fori_loop(0, tiles, first, 0)

    def second(t, _):
        keep[t] = jnp.dot(
            post[mybits[0]], normed[:, cols(t)], preferred_element_type=jnp.float32)
        return 0

    lax.fori_loop(0, tiles, second, 0)

    def absorb(j, t):
        stage_copy(j, t).wait_recv()
        size = half0 >> (j + 1)
        there = pl.ds(pl.multiple_of((1 - (mybits[j + 1] if j + 1 < nr else k)) * size, 16), size)
        here = pl.ds(pl.multiple_of((mybits[j + 1] if j + 1 < nr else k) * size, 16), size)
        gone = keep[t, there, :] + recvs[j][t, there, :].astype(jnp.float32)
        if j + 1 < nr:
            sends[j + 1][t] = gone.astype(jnp.bfloat16)
            stage_copy(j + 1, t).start()
        else:
            last[t] = gone
            last_copy(t).start()
        held = keep[t, here, :] + recvs[j][t, here, :].astype(jnp.float32)
        if j + 1 < nr:
            keep[t, 0:size, :] = held
        else:
            out[:, pl.ds(pl.multiple_of(k * q + t * w, 128), w)] = held

    for t in range(tiles + nr - 1):
        for j in range(nr):
            if 0 <= t - j < tiles:
                absorb(j, t - j)

    def finish(t, _):
        last_copy(t).wait()
        for j in range(nr):
            stage_copy(j, t).wait_send()
        return 0

    lax.fori_loop(0, tiles, finish, 0)


def view_sum_blocks(n, post, normed, block_rows):
    bits = image_bits(n)
    nr = len(bits)
    q = normed.shape[1]
    tiles = 8
    w = q // tiles
    half0 = post.shape[1]
    vm = pl.BlockSpec(memory_space=pltpu.VMEM)
    moving = [pltpu.VMEM((tiles, half0 >> j, w), jnp.bfloat16) for j in range(nr)]
    return pl.pallas_call(
        functools.partial(sums_kernel, n, tiles),
        out_shape=jax.ShapeDtypeStruct((block_rows, 2 * q), jnp.float32),
        in_specs=[vm, vm],
        out_specs=vm,
        scratch_shapes=[pltpu.VMEM((tiles, half0, w), jnp.float32)] + moving + moving + [
            pltpu.VMEM((tiles, block_rows, w), jnp.float32),
            pltpu.SemaphoreType.DMA((nr + 1, tiles)),
            pltpu.SemaphoreType.DMA((nr + 1, tiles)),
        ],
        compiler_params=pltpu.CompilerParams(
            collective_id=1, has_side_effects=True, vmem_limit_bytes=56 * 2**20),
    )(post, normed)


def pair_perm(n, value):
    return [(i, i ^ value) for i in range(n)]


def on_device(images, references, cycle_mask, view_class):
    n = lax.axis_size("img")
    m = lax.axis_size("pix")
    d = lax.axis_index("img")
    k, c = bit(d, PIXEL_BIT), bit(d, VIEW_BIT)
    bits = image_bits(n)
    nr = len(bits)
    rows, pixels = images.shape
    q = pixels // 2
    nviews = references.shape[0]
    total_images = rows * n

    widened = images.astype(jnp.float32)
    col_sum, col_sq = lax.psum((jnp.sum(widened, 0), jnp.sum(widened * widened, 0)), "img")
    img_all, ref_all = gather(n, images, references)

    def quarter(x):
        return lax.dynamic_slice_in_dim(x, k * q, q)

    pix_mean = quarter(col_sum) / total_images
    pix_std = jnp.sqrt(quarter(col_sq) / total_images - pix_mean * pix_mean + EPSILON)
    weight = quarter(cycle_mask).astype(jnp.float32)
    img_all = img_all.reshape(4 * rows, q)
    whitened = (img_all.astype(jnp.float32) - pix_mean) / pix_std
    parts = jnp.concatenate([
        jnp.sum(whitened * weight, 1),
        jnp.sum(whitened * whitened * weight, 1),
        jnp.broadcast_to(jnp.sum(weight), (128,)),
    ])
    parts = lax.psum(parts, "pix")
    parts = parts + lax.ppermute(parts, "img", pair_perm(n, PIXEL_BIT))
    count = parts[-1]
    bg_mean = parts[:4 * rows] / count
    bg_std = jnp.sqrt(parts[4 * rows:8 * rows] / count - bg_mean * bg_mean + EPSILON)
    normed = ((whitened - bg_mean[:, None]) / bg_std[:, None]).astype(jnp.bfloat16)

    views = ref_all.reshape(-1, q)
    energy = jnp.sum(jnp.square(views.astype(jnp.float32)), 1)
    raw = lax.dot_general(
        normed, views, (((1,), (1,)), ((), ())), preferred_element_type=jnp.float32)
    partial_value = (raw - 0.5 * energy[None, :]).reshape(4, rows, -1)
    share = lax.psum_scatter(partial_value, "pix", scatter_dimension=1, tiled=True)
    scores = (share + lax.ppermute(share, "img", pair_perm(n, PIXEL_BIT))) * (4.0 / SIDE)

    row_max = jnp.max(scores, 2)
    row_exp = jnp.sum(jnp.exp(scores - row_max[..., None]), 2)
    row_sum = jnp.sum(scores, 2)
    here = jnp.stack([row_max, row_exp, row_sum])
    there = lax.ppermute(here, "img", pair_perm(n, VIEW_BIT))
    both_max = jnp.maximum(here[0], there[0])
    both_exp = here[1] * jnp.exp(here[0] - both_max) + there[1] * jnp.exp(there[0] - both_max)
    log_total = both_max + jnp.log(both_exp)
    nref = nviews * n
    evidence = log_total - (here[2] + there[2]) / nref
    evidence = lax.dynamic_index_in_dim(evidence, 2 * c + k, 0, keepdims=False)
    posterior = jnp.exp(scores - log_total[..., None]).astype(jnp.bfloat16)
    posterior = lax.all_gather(posterior, "pix", axis=1, tiled=True)
    posterior = posterior.reshape(4 * rows, -1)

    normed = lax.optimization_barrier(normed)
    view_sums = view_sum_blocks(n, posterior.T.reshape(2, -1, 4 * rows), normed, nviews)

    class_mass = jnp.sum(posterior, 0, dtype=jnp.float32).reshape(n // 2, nviews)
    slots = jnp.arange(n // 2)
    owner = (slots % 2) * PIXEL_BIT + c * VIEW_BIT
    for j, b in enumerate(bits):
        owner = owner + ((slots // 2 ** (nr - j)) % 2) * b
    classes = view_class.reshape(n, nviews)[owner]
    onehot = (classes.reshape(-1)[:, None] == jnp.arange(NCLS, dtype=jnp.int32)[None, :]).astype(jnp.float32)
    class_local = jnp.dot(class_mass.reshape(-1), onehot, precision=lax.Precision.HIGHEST)
    class_total = 0.5 * lax.psum(class_local, "img")
    return (view_sums, class_total * (NCLS / total_images), evidence.reshape(-1))


def solution(mesh):
    in_specs = (P("img", "pix"), P("img", "pix"), P("pix"), P())
    out_specs = (P("img", "pix"), P(), P(("img", "pix")))
    return jax.shard_map(
        on_device, mesh=mesh, in_specs=in_specs, out_specs=out_specs, check_vma=False
    )
```

```python
import functools

import jax
import jax.numpy as jnp
from jax import lax
from jax.experimental import pallas as pl
from jax.experimental.pallas import tpu as pltpu
from jax.sharding import PartitionSpec as P

SIDE = 128
NCLS = 96
EPSILON = 1e-05
MESH = pl.DeviceIdType.MESH
F32 = jnp.float32
BF16 = jnp.bfloat16

PIXEL_BIT = 4
VIEW_BIT = 2
CHUNKS = 4
TILES = 8


def image_bits(n):
    return [b for b in (1, *reversed([2**j for j in range(3, 20) if 2**j < n]))]


def low_bits(m):
    return [2**j for j in range(20) if 2**j < m]


def bit(index, value):
    return (index // value) % 2


def flip(index, value):
    return index + value * (1 - 2 * bit(index, value))


def aligned(start, size, unit):
    return pl.ds(pl.multiple_of(start, unit), size)


def kernel(n, m, images, refs, mask, classes, out, ev_out, cls_out,
           img_all, pair_img, ref_all, stat, stat_in, col, bg, bg_mine, bg_in,
           ecol, erow, partial, halves, soft, soft_in, evb, post, post_t,
           mass, mass_in, fresh, keep, sends, recvs, last,
           lsem, isend, irecv, rsend, rrecv, tsend, trecv, bsend, brecv,
           hsend, hrecv, csend, crecv, gsend, grecv, vsend, vrecv, ksend, krecv,
           esend, erecv):
    d = lax.axis_index("img")
    p = lax.axis_index("pix")
    bits = image_bits(n)
    nr = len(bits)
    pbits = list(reversed(low_bits(m)))
    k, c = bit(d, PIXEL_BIT), bit(d, VIEW_BIT)
    kp, cp = flip(d, PIXEL_BIT), flip(d, VIEW_BIT)
    rows, cols = images.shape
    nviews = refs.shape[0]
    q = cols // 2
    mine = aligned(k * q, q, 128)
    theirs = aligned((1 - k) * q, q, 128)
    weights = [2 ** (nr - j) for j in range(nr)]
    slot = k
    for b, w in zip(bits, weights):
        slot = slot + w * bit(d, b)
    own = 2 * c + k
    other = 2 * c + 1 - k
    across = 2 * (1 - c) + k
    diag = 2 * (1 - c) + 1 - k

    barrier = pltpu.get_barrier_semaphore()
    img_partners = [kp, cp] + [flip(d, b) for b in bits]
    for x in img_partners:
        pl.semaphore_signal(barrier, inc=1, device_id={"img": x}, device_id_type=MESH)
    for b in pbits:
        pl.semaphore_signal(barrier, inc=1, device_id={"pix": flip(p, b)}, device_id_type=MESH)
    pl.semaphore_wait(barrier, len(img_partners) + len(pbits))

    def remote(src, dst, ssem, rsem, axis, partner):
        return pltpu.make_async_remote_copy(
            src_ref=src, dst_ref=dst, send_sem=ssem, recv_sem=rsem,
            device_id={axis: partner}, device_id_type=MESH)

    ref_copies = []
    img_copies = []
    waited = []

    def send_ref(src, s, partner):
        i = len(ref_copies)
        x = remote(src, ref_all.at[s], rsend.at[i], rrecv.at[i], "img", partner)
        x.start()
        ref_copies.append(x)
        return x

    def send_img(src, dst, partner):
        i = len(img_copies)
        x = remote(src, dst, isend.at[i], irecv.at[i], "img", partner)
        x.start()
        img_copies.append(x)
        return x

    def arrive(x):
        if all(x is not y for y in waited):
            x.wait_recv()
            waited.append(x)

    step = rows // CHUNKS

    def chunk(i):
        return pl.ds(i * step, step)

    order = list(reversed(list(zip(bits, weights))))
    pair_ref = send_ref(refs.at[:, theirs], slot, kp)
    stage = [[] for _ in order]
    for j, (b, w) in enumerate(order):
        stage[j].append((send_ref(refs.at[:, mine], slot, flip(d, b)), slot))
    img_across = send_img(images.at[:, mine], img_all.at[own], cp)
    own_ref = pltpu.make_async_copy(refs.at[:, mine], ref_all.at[slot], lsem.at[0])
    own_ref.start()

    wide = min(512, cols)

    def col_tile(t, _):
        at = aligned(t * wide, wide, 128)
        x = images[:, at].astype(F32)
        stat[0, 0:1, at] = jnp.sum(x, 0, keepdims=True)
        stat[0, 1:2, at] = jnp.sum(x * x, 0, keepdims=True)
        return 0

    lax.fori_loop(0, cols // wide, col_tile, 0)
    img_k = []
    hops = [*bits, VIEW_BIT, PIXEL_BIT]
    for j, b in enumerate(hops):
        x = remote(stat.at[j], stat_in.at[j], tsend.at[j], trecv.at[j], "img", flip(d, b))
        x.start()
        x.wait()
        stat[j + 1] = stat[j] + stat_in[j]
        if j == 1:
            img_k.append(send_img(images.at[chunk(0), theirs], pair_img.at[chunk(0)], kp))
    total = rows * n
    nh = len(hops)
    col_mean = stat[nh, 0:1, :] / total
    col[0:1, :] = col_mean
    col[1:2, :] = 1.0 / jnp.sqrt(stat[nh, 1:2, :] / total - col_mean * col_mean + EPSILON)

    arrive(pair_ref)
    pair_slot = slot + 1 - 2 * k
    for j, (b, w) in enumerate(order):
        stage[j].append((send_ref(ref_all.at[pair_slot], pair_slot, flip(d, b)), pair_slot))
    img_k.append(send_img(images.at[chunk(1), theirs], pair_img.at[chunk(1)], kp))

    def bg_tile(t, carry):
        s, sq, cnt = carry
        at = aligned(t * wide, wide, 128)
        w = (images[:, at].astype(F32) - col[0:1, at]) * col[1:2, at]
        mk = mask[:, at].astype(F32)
        wm = w * mk
        wq = wm * w
        for i in range(wide // 128):
            part = slice(i * 128, (i + 1) * 128)
            s = s + wm[:, part]
            sq = sq + wq[:, part]
            cnt = cnt + mk[:, part]
        return s, sq, cnt

    zero = jnp.zeros((rows, 128), F32)
    s, sq, cnt = lax.fori_loop(0, cols // wide, bg_tile, (zero, zero, jnp.zeros((1, 128), F32)))
    lane = lax.broadcasted_iota(jnp.int32, (rows, 128), 1)
    bg_mine[0] = jnp.where(
        lane == 0, jnp.sum(s, 1, keepdims=True),
        jnp.where(lane == 1, jnp.sum(sq, 1, keepdims=True), jnp.sum(cnt, 1, keepdims=True)))
    for j, b in enumerate(pbits):
        x = remote(bg_mine.at[j], bg_in.at[j], bsend.at[j], brecv.at[j], "pix", flip(p, b))
        x.start()
        x.wait()
        bg_mine[j + 1] = bg_mine[j] + bg_in[j]
    np_ = len(pbits)
    sums = bg_mine[np_]
    count = sums[:, 2:3]
    bg_mean = sums[:, 0:1] / count
    bg_inv = 1.0 / jnp.sqrt(sums[:, 1:2] / count - bg_mean * bg_mean + EPSILON)
    bg[own] = jnp.where(lane == 0, bg_mean, bg_inv)
    bg_k = remote(bg.at[own], bg.at[own], bsend.at[np_], brecv.at[np_], "img", kp)
    bg_k.start()
    bg_c = remote(bg.at[own], bg.at[own], bsend.at[np_ + 1], brecv.at[np_ + 1], "img", cp)
    bg_c.start()

    ncol = min(512, q)

    def normalise(read, s):
        def tile(t, _):
            at = aligned(t * ncol, ncol, 128)
            there = aligned(k * q + t * ncol, ncol, 128)
            w = (read(t, at, there).astype(F32) - col[0:1, there]) * col[1:2, there]
            img_all[s, :, at] = ((w - bg[s, :, 0:1]) * bg[s, :, 1:2]).astype(BF16)
            return 0
        lax.fori_loop(0, q // ncol, tile, 0)

    normalise(lambda t, at, there: images[:, there], own)

    def energy(s):
        def tile(t, acc):
            x = ref_all[s, :, aligned(t * ncol, ncol, 128)].astype(F32)
            x = x * x
            for i in range(ncol // 128):
                acc = acc + x[:, i * 128:(i + 1) * 128]
            return acc
        acc = lax.fori_loop(0, q // ncol, tile, jnp.zeros((nviews, 128), F32))
        ecol[s] = jnp.broadcast_to(jnp.sum(acc, 1, keepdims=True), (nviews, 128))

    bg_k.wait_recv()
    bg_d = remote(bg.at[other], bg.at[other], bsend.at[np_ + 2], brecv.at[np_ + 2], "img", cp)
    bg_d.start()

    sent_k = [2]

    def next_k():
        i = sent_k[0]
        if i < CHUNKS:
            img_k.append(send_img(images.at[chunk(i), theirs], pair_img.at[chunk(i)], kp))
            sent_k[0] += 1

    fwd = []

    def forward_img():
        i = len(fwd)
        if i < CHUNKS:
            arrive(img_k[i])
            fwd.append(send_img(pair_img.at[chunk(i)], img_all.at[other, chunk(i)], cp))
            next_k()

    for j, (b, w) in enumerate(order[:-1]):
        for x, s in stage[j]:
            arrive(x)
            got = s + w * (1 - 2 * bit(d, b))
            for j2 in range(j + 1, len(order)):
                stage[j2].append((send_ref(ref_all.at[got], got, flip(d, order[j2][0])), got))
            forward_img()
    while len(fwd) < CHUNKS:
        forward_img()
    normalise(lambda t, at, there: pair_img[:, at], other)
    own_ref.wait()
    energy(slot)
    energy(pair_slot)
    for j, (b, w) in enumerate(order):
        for x, s in stage[j]:
            arrive(x)
            energy(s + w * (1 - 2 * bit(d, b)))
    erow[...] = jnp.transpose(ecol[...].reshape(-1, 128))[0:8]

    nv = nviews * n // 2
    kt = min(1024, q)

    def score(s):
        partial[s] = jnp.broadcast_to(-0.5 * erow[0:1, :], (rows, nv))

        def tile(t, _):
            at = aligned(t * kt, kt, 128)
            partial[s] += lax.dot_general(
                img_all[s, :, at], ref_all[:, :, at].reshape(nv, kt),
                (((1,), (1,)), ((), ())), preferred_element_type=F32)
            return 0
        lax.fori_loop(0, q // kt, tile, 0)

    cuts = [("pix", b, flip(p, b), bit(p, b)) for b in pbits] + [("img", PIXEL_BIT, kp, k)]
    nc = len(cuts)
    starts, sizes = [0], [rows]
    for axis, b, partner, mybit in cuts:
        sizes.append(sizes[-1] // 2)
        starts.append(starts[-1] + mybit * sizes[-1])

    def halve(j, s):
        axis, b, partner, mybit = cuts[j]
        gone = aligned(starts[j] + (1 - mybit) * sizes[j + 1], sizes[j + 1], sizes[j + 1])
        return remote(partial.at[s, gone], halves[j].at[s], hsend.at[j, s], hrecv.at[j, s], axis, partner)

    def absorb_half(j, s):
        halve(j, s).wait_recv()
        held = aligned(starts[j + 1], sizes[j + 1], sizes[j + 1])
        partial[s, held, :] += halves[j][s]

    def slot_of(i):
        return 2 * ((c + i // 2) % 2) + i % 2

    def begin(i, _):
        s = slot_of(i)
        score(s)
        halve(0, s).start()
        return 0

    def middle(j):
        def body(i, _):
            s = slot_of(i)
            absorb_half(j, s)
            halve(j + 1, s).start()
            return 0
        return body

    nlast = sizes[-1]
    held = aligned(starts[-1], nlast, nlast)
    lane2 = lax.broadcasted_iota(jnp.int32, (nlast, 128), 1)

    def soft_copy(s):
        return remote(soft.at[s], soft_in.at[s], csend.at[s], crecv.at[s], "img", cp)

    def soften(i, _):
        s = slot_of(i)
        absorb_half(nc - 1, s)
        x = partial[s, held, :] * (4.0 / SIDE)
        partial[s, held, :] = x
        top = jnp.max(x, 1, keepdims=True)
        soft[s] = jnp.where(
            lane2 == 0, top,
            jnp.where(lane2 == 1, jnp.sum(jnp.exp(x - top), 1, keepdims=True),
                      jnp.sum(x, 1, keepdims=True)))
        soft_copy(s).start()
        return 0

    def grow(j, s):
        axis, b, partner, mybit = cuts[j]
        at = aligned(starts[j + 1], sizes[j + 1], sizes[j + 1])
        return remote(post.at[s, at], post.at[s, at], gsend.at[j, s], grecv.at[j, s], axis, partner)

    def settle(i, _):
        s = slot_of(i)
        soft_copy(s).wait_recv()
        a, b = soft[s], soft_in[s]
        top = jnp.maximum(a[:, 0:1], b[:, 0:1])
        exps = a[:, 1:2] * jnp.exp(a[:, 0:1] - top) + b[:, 1:2] * jnp.exp(b[:, 0:1] - top)
        log_total = top + jnp.log(exps)
        evb[s] = jnp.broadcast_to(
            log_total - (a[:, 2:3] + b[:, 2:3]) / (nviews * n), (nlast, 128))
        post[s, held, :] = jnp.exp(partial[s, held, :] - log_total).astype(BF16)
        grow(nc - 1, s).start()
        return 0

    lax.fori_loop(0, 2, begin, 0)
    for j in range(nc - 1):
        lax.fori_loop(0, 2, middle(j), 0)
    bg_c.wait_recv()
    arrive(img_across)
    normalise(lambda t, at, there: img_all[across, :, at], across)
    bg_d.wait_recv()
    for x in fwd:
        arrive(x)
    normalise(lambda t, at, there: img_all[diag, :, at], diag)
    lax.fori_loop(2, 4, begin, 0)
    lax.fori_loop(0, 2, soften, 0)
    for j in range(nc - 1):
        lax.fori_loop(2, 4, middle(j), 0)
    lax.fori_loop(2, 4, soften, 0)
    lax.fori_loop(0, 4, settle, 0)
    for j in range(nc - 1, 0, -1):
        def grown(i, _, j=j):
            s = slot_of(i)
            grow(j, s).wait_recv()
            grow(j - 1, s).start()
            return 0
        lax.fori_loop(0, 4, grown, 0)

    half0 = nv // 2

    def turn(i, acc):
        s = slot_of(i)
        grow(0, s).wait_recv()
        x = post[s].astype(F32)
        xt = jnp.transpose(x).astype(BF16)
        at = aligned(s * rows, rows, 128)
        post_t[0, :, at] = xt[:half0]
        post_t[1, :, at] = xt[half0:]
        return acc + jnp.sum(x, 0, keepdims=True)

    class_mass = lax.fori_loop(0, 4, turn, jnp.zeros((1, nv), F32))

    wt = q // TILES
    partners = [flip(d, b) for b in bits]
    mybits = [bit(d, b) for b in bits] + [k]

    def tile_cols(t):
        return aligned(t * wt, wt, 128)

    def weigh(half, t):
        return jnp.dot(post_t[half], img_all[:, :, tile_cols(t)].reshape(4 * rows, wt),
                       preferred_element_type=F32)

    def stage_copy(j, t):
        return remote(sends[j].at[t], recvs[j].at[t], vsend.at[j, t], vrecv.at[j, t],
                      "img", partners[j])

    def last_copy(t):
        place = aligned(k * q + t * wt, wt, 128)
        return remote(last.at[t], out.at[:, place], vsend.at[nr, t], vrecv.at[nr, t], "img", kp)

    def first(t, _):
        sends[0][t] = weigh(1 - mybits[0], t).astype(BF16)
        stage_copy(0, t).start()
        return 0

    lax.fori_loop(0, TILES, first, 0)

    ev_out[aligned(k * nlast, nlast, nlast), :] = evb[own]
    ev_copy = remote(evb.at[other], ev_out.at[aligned(k * nlast, nlast, nlast)],
                     esend.at[0], erecv.at[0], "img", kp)
    ev_copy.start()

    hit = lax.broadcasted_iota(jnp.int32, (NCLS, nv), 0) == classes[...]
    mass[0] = jnp.broadcast_to(
        jnp.sum(jnp.where(hit, class_mass, 0.0), 1, keepdims=True), (NCLS, 128))
    mass_hops = [*bits, VIEW_BIT]

    def mass_copy(j):
        return remote(mass.at[j], mass_in.at[j], ksend.at[j], krecv.at[j], "img", flip(d, mass_hops[j]))

    mass_copy(0).start()

    def mass_hop(j):
        if j < len(mass_hops):
            mass_copy(j).wait()
            mass[j + 1] = mass[j] + mass_in[j]
            if j + 1 < len(mass_hops):
                mass_copy(j + 1).start()

    def absorb(j, t):
        size = half0 >> (j + 1)
        there = aligned((1 - mybits[j + 1]) * size, size, 16)
        here = aligned(mybits[j + 1] * size, size, 16)
        if j == 0:
            fresh[...] = weigh(mybits[0], t)
            base = fresh
        else:
            base = keep[j - 1].at[t]
        stage_copy(j, t).wait_recv()
        gone = base[there, :] + recvs[j][t, there, :].astype(F32)
        if j + 1 < nr:
            sends[j + 1][t] = gone.astype(BF16)
            stage_copy(j + 1, t).start()
        else:
            last[t] = gone
            last_copy(t).start()
        rest = base[here, :] + recvs[j][t, here, :].astype(F32)
        if j + 1 < nr:
            keep[j][t] = rest
        else:
            out[:, aligned(k * q + t * wt, wt, 128)] = rest

    def steps(t):
        for j in range(nr):
            absorb(j, t - j)

    def ramp(ts):
        for t in ts:
            for j in range(nr):
                if 0 <= t - j < TILES:
                    absorb(j, t - j)

    ramp(range(nr - 1))
    mass_hop(0)
    lax.fori_loop(nr - 1, TILES // 2, lambda t, _: (steps(t), 0)[1], 0)
    mass_hop(1)
    lax.fori_loop(TILES // 2, TILES, lambda t, _: (steps(t), 0)[1], 0)
    for j in range(2, len(mass_hops)):
        mass_hop(j)
    cls_out[...] = mass[len(mass_hops)] * (NCLS / total)
    ramp(range(TILES, TILES + nr - 1))

    for x in ref_copies + img_copies + [bg_k, bg_c, bg_d]:
        x.wait_send()
    ev_copy.wait()

    def drain(s, _):
        soft_copy(s).wait_send()
        for j in range(nc):
            halve(j, s).wait_send()
            grow(j, s).wait_send()
        return 0

    lax.fori_loop(0, 4, drain, 0)

    def finish(t, _):
        last_copy(t).wait()
        for j in range(nr):
            stage_copy(j, t).wait_send()
        return 0

    lax.fori_loop(0, TILES, finish, 0)


def whole_step(n, m, images, refs, mask, classes):
    rows, cols = images.shape
    nviews = refs.shape[0]
    q = cols // 2
    bits = image_bits(n)
    nr = len(bits)
    nb = nr + 2
    npix = len(low_bits(m))
    nc = npix + 1
    nv = nviews * n // 2
    half0 = nv // 2
    wt = q // TILES
    nlast = rows >> nc
    n_ref = 1 + sum(2 ** (j + 1) for j in range(nr))
    n_img = 1 + 2 * CHUNKS
    vm = pl.BlockSpec(memory_space=pltpu.VMEM)
    hbm = pl.BlockSpec(memory_space=pl.ANY)
    V = pltpu.VMEM
    dma = pltpu.SemaphoreType.DMA
    scratch = [
        V((4, rows, q), BF16), V((rows, q), BF16), V((n // 2, nviews, q), BF16),
        V((nb + 1, 2, cols), F32), V((nb, 2, cols), F32), V((2, cols), F32),
        V((4, rows, 128), F32), V((npix + 1, rows, 128), F32), V((npix, rows, 128), F32),
        V((n // 2, nviews, 128), F32), V((8, nv), F32),
        V((4, rows, nv), F32), [V((4, rows >> (j + 1), nv), F32) for j in range(nc)],
        V((4, nlast, 128), F32), V((4, nlast, 128), F32), V((4, nlast, 128), F32),
        V((4, rows, nv), BF16), V((2, half0, 4 * rows), BF16),
        V((nb, NCLS, 128), F32), V((nb - 1, NCLS, 128), F32),
        V((half0, wt), F32),
        [V((TILES, half0 >> (j + 1), wt), F32) for j in range(nr - 1)],
        [V((TILES, half0 >> j, wt), BF16) for j in range(nr)],
        [V((TILES, half0 >> j, wt), BF16) for j in range(nr)],
        V((TILES, nviews, wt), F32),
        dma((1,)), dma((n_img,)), dma((n_img,)), dma((n_ref,)), dma((n_ref,)),
        dma((nb,)), dma((nb,)), dma((npix + 3,)), dma((npix + 3,)),
        dma((nc, 4)), dma((nc, 4)), dma((4,)), dma((4,)), dma((nc, 4)), dma((nc, 4)),
        dma((nr + 1, TILES)), dma((nr + 1, TILES)), dma((nb - 1,)), dma((nb - 1,)),
        dma((1,)), dma((1,)),
    ]
    return pl.pallas_call(
        functools.partial(kernel, n, m),
        out_shape=(
            jax.ShapeDtypeStruct((nviews, cols), F32),
            jax.ShapeDtypeStruct((rows // m, 128), F32),
            jax.ShapeDtypeStruct((NCLS, 128), F32),
        ),
        in_specs=[vm, hbm, vm, vm],
        out_specs=(vm, vm, vm),
        scratch_shapes=scratch,
        compiler_params=pltpu.CompilerParams(
            collective_id=0, has_side_effects=True, vmem_limit_bytes=62 * 2**20),
    )(images, refs, mask, classes)


def on_device(images, references, cycle_mask, view_class):
    n = lax.axis_size("img")
    m = lax.axis_size("pix")
    c = bit(lax.axis_index("img"), VIEW_BIT)
    nviews = references.shape[0]
    bits = image_bits(n)
    nr = len(bits)
    owner = []
    for slot in range(n // 2):
        at = (slot % 2) * PIXEL_BIT
        for j, b in enumerate(bits):
            at = at + ((slot // 2 ** (nr - j)) % 2) * b
        owner.append(at)
    by_owner = view_class.reshape(n, nviews)
    groups = [
        jnp.concatenate([by_owner[at + g * VIEW_BIT] for at in owner]) for g in range(2)
    ]
    classes = jnp.where(c == 0, groups[0], groups[1])[None, :]
    view_sums, evidence, class_share = whole_step(
        n, m, images, references, cycle_mask[None, :], classes)
    return (view_sums, class_share[:, 0], evidence[:, 0])


def solution(mesh):
    in_specs = (P("img", "pix"), P("img", "pix"), P("pix"), P())
    out_specs = (P("img", "pix"), P(), P(("img", "pix")))
    return jax.shard_map(
        on_device, mesh=mesh, in_specs=in_specs, out_specs=out_specs, check_vma=False
    )
```

```python
import functools

import jax
import jax.numpy as jnp
from jax import lax
from jax.experimental import pallas as pl
from jax.experimental.pallas import tpu as pltpu
from jax.sharding import PartitionSpec as P

SIDE = 128
NCLS = 96
EPSILON = 1e-05
MESH = pl.DeviceIdType.MESH
F32 = jnp.float32
BF16 = jnp.bfloat16

PIXEL_BIT = 4
VIEW_BIT = 2
CHUNKS = 4


def image_bits(n):
    return [b for b in (1, *reversed([2**j for j in range(3, 20) if 2**j < n]))]


def low_bits(m):
    return [2**j for j in range(20) if 2**j < m]


def pixel_tiles(q):
    return min(16, q // 128)


def bit(index, value):
    return (index // value) % 2


def flip(index, value):
    return index + value * (1 - 2 * bit(index, value))


def aligned(start, size, unit):
    return pl.ds(pl.multiple_of(start, unit), size)


def kernel(n, m, images, refs, mask, classes, out, ev_out, cls_out,
           img_all, pair_img, ref_all, stat, stat_in, col, bg, bg_mine, bg_in,
           ecol, erow, partial, halves, soft, soft_in, evb, ev_all, post, post_t,
           mass, mass_in, fresh, keep, sends, recvs, last,
           lsem, isend, irecv, rsend, rrecv, tsend, trecv, bsend, brecv,
           hsend, hrecv, csend, crecv, gsend, grecv, vsend, vrecv, ksend, krecv,
           esend, erecv):
    d = lax.axis_index("img")
    p = lax.axis_index("pix")
    bits = image_bits(n)
    nr = len(bits)
    pbits = list(reversed(low_bits(m)))
    k, c = bit(d, PIXEL_BIT), bit(d, VIEW_BIT)
    kp, cp = flip(d, PIXEL_BIT), flip(d, VIEW_BIT)
    rows, cols = images.shape
    nviews = refs.shape[0]
    q = cols // 2
    mine = aligned(k * q, q, 128)
    theirs = aligned((1 - k) * q, q, 128)
    weights = [2 ** (nr - j) for j in range(nr)]
    slot = k
    for b, w in zip(bits, weights):
        slot = slot + w * bit(d, b)
    own = 2 * c + k
    other = 2 * c + 1 - k
    across = 2 * (1 - c) + k
    diag = 2 * (1 - c) + 1 - k

    barrier = pltpu.get_barrier_semaphore()
    img_partners = [kp, cp] + [flip(d, b) for b in bits]
    for x in img_partners:
        pl.semaphore_signal(barrier, inc=1, device_id={"img": x}, device_id_type=MESH)
    for b in pbits:
        pl.semaphore_signal(barrier, inc=1, device_id={"pix": flip(p, b)}, device_id_type=MESH)
    pl.semaphore_wait(barrier, len(img_partners) + len(pbits))

    def remote(src, dst, ssem, rsem, axis, partner):
        return pltpu.make_async_remote_copy(
            src_ref=src, dst_ref=dst, send_sem=ssem, recv_sem=rsem,
            device_id={axis: partner}, device_id_type=MESH)

    ref_copies = []
    img_copies = []
    waited = []

    def send_ref(src, s, partner):
        i = len(ref_copies)
        x = remote(src, ref_all.at[s], rsend.at[i], rrecv.at[i], "img", partner)
        x.start()
        ref_copies.append(x)
        return x

    def send_img(src, dst, partner):
        i = len(img_copies)
        x = remote(src, dst, isend.at[i], irecv.at[i], "img", partner)
        x.start()
        img_copies.append(x)
        return x

    def arrive(x):
        if all(x is not y for y in waited):
            x.wait_recv()
            waited.append(x)

    step = rows // CHUNKS

    def chunk(i):
        return pl.ds(i * step, step)

    order = list(reversed(list(zip(bits, weights))))
    pair_ref = send_ref(refs.at[:, theirs], slot, kp)
    stage = [[] for _ in order]

    def spread(src, s, first, stop):
        for j in range(first, stop):
            stage[j].append((send_ref(src, s, flip(d, order[j][0])), s))

    far = len(order) - 1
    spread(refs.at[:, mine], slot, far, far + 1)
    img_across = []

    def send_across(i):
        img_across.append(send_img(images.at[chunk(i), mine], img_all.at[own, chunk(i)], cp))

    send_across(0)
    own_ref = pltpu.make_async_copy(refs.at[:, mine], ref_all.at[slot], lsem.at[0])
    own_ref.start()

    wide = min(512, cols)

    def col_tile(t, _):
        at = aligned(t * wide, wide, 128)
        x = images[:, at].astype(F32)
        stat[0, 0:1, at] = jnp.sum(x, 0, keepdims=True)
        stat[0, 1:2, at] = jnp.sum(x * x, 0, keepdims=True)
        return 0

    lax.fori_loop(0, cols // wide, col_tile, 0)
    hops = [PIXEL_BIT, *[b for b, _ in order[:-1]], VIEW_BIT, order[-1][0]]

    def hop(j):
        x = remote(stat.at[j], stat_in.at[j], tsend.at[j], trecv.at[j], "img", flip(d, hops[j]))
        x.start()
        x.wait()
        stat[j + 1] = stat[j] + stat_in[j]

    img_k = []

    def send_pair(i):
        img_k.append(send_img(images.at[chunk(i), theirs], pair_img.at[chunk(i)], kp))

    for j in range(len(order)):
        hop(j)
    spread(refs.at[:, mine], slot, 0, far)
    arrive(pair_ref)
    pair_slot = slot + 1 - 2 * k
    spread(ref_all.at[pair_slot], pair_slot, 0, far)
    for i in range(CHUNKS - 1):
        send_pair(i)
    for j in range(len(order), len(hops)):
        hop(j)
    for i in range(1, CHUNKS):
        send_across(i)
    spread(ref_all.at[pair_slot], pair_slot, far, far + 1)
    total = rows * n
    nh = len(hops)
    col_mean = stat[nh, 0:1, :] / total
    col[0:1, :] = col_mean
    col[1:2, :] = 1.0 / jnp.sqrt(stat[nh, 1:2, :] / total - col_mean * col_mean + EPSILON)

    def bg_tile(t, carry):
        s, sq, cnt = carry
        at = aligned(t * wide, wide, 128)
        w = (images[:, at].astype(F32) - col[0:1, at]) * col[1:2, at]
        mk = mask[:, at].astype(F32)
        wm = w * mk
        wq = wm * w
        for i in range(wide // 128):
            part = slice(i * 128, (i + 1) * 128)
            s = s + wm[:, part]
            sq = sq + wq[:, part]
            cnt = cnt + mk[:, part]
        return s, sq, cnt

    zero = jnp.zeros((rows, 128), F32)
    s, sq, cnt = lax.fori_loop(0, cols // wide, bg_tile, (zero, zero, jnp.zeros((1, 128), F32)))
    lane = lax.broadcasted_iota(jnp.int32, (rows, 128), 1)
    bg_mine[0] = jnp.where(
        lane == 0, jnp.sum(s, 1, keepdims=True),
        jnp.where(lane == 1, jnp.sum(sq, 1, keepdims=True), jnp.sum(cnt, 1, keepdims=True)))
    for j, b in enumerate(pbits):
        x = remote(bg_mine.at[j], bg_in.at[j], bsend.at[j], brecv.at[j], "pix", flip(p, b))
        x.start()
        x.wait()
        bg_mine[j + 1] = bg_mine[j] + bg_in[j]
    np_ = len(pbits)
    sums = bg_mine[np_]
    count = sums[:, 2:3]
    bg_mean = sums[:, 0:1] / count
    bg_inv = 1.0 / jnp.sqrt(sums[:, 1:2] / count - bg_mean * bg_mean + EPSILON)
    bg[own] = jnp.where(lane == 0, bg_mean, bg_inv)
    bg_k = remote(bg.at[own], bg.at[own], bsend.at[np_], brecv.at[np_], "img", kp)
    bg_k.start()
    send_pair(CHUNKS - 1)
    bg_c = remote(bg.at[own], bg.at[own], bsend.at[np_ + 1], brecv.at[np_ + 1], "img", cp)
    bg_c.start()

    ncol = min(512, q)

    def normalise(read, s, r=pl.ds(0, rows)):
        def tile(t, _):
            at = aligned(t * ncol, ncol, 128)
            there = aligned(k * q + t * ncol, ncol, 128)
            w = (read(at, there).astype(F32) - col[0:1, there]) * col[1:2, there]
            img_all[s, r, at] = ((w - bg[s, r, 0:1]) * bg[s, r, 1:2]).astype(BF16)
            return 0
        lax.fori_loop(0, q // ncol, tile, 0)

    def energy(s):
        def tile(t, acc):
            x = ref_all[s, :, aligned(t * ncol, ncol, 128)].astype(F32)
            x = x * x
            for i in range(ncol // 128):
                acc = acc + x[:, i * 128:(i + 1) * 128]
            return acc
        acc = lax.fori_loop(0, q // ncol, tile, jnp.zeros((nviews, 128), F32))
        ecol[s] = jnp.broadcast_to(jnp.sum(acc, 1, keepdims=True), (nviews, 128))

    for j, (b, w) in enumerate(order[:-1]):
        for x, s in stage[j]:
            arrive(x)
            got = s + w * (1 - 2 * bit(d, b))
            spread(ref_all.at[got], got, j + 1, len(order))
            if len(stage[0]) and x is stage[0][0][0]:
                normalise(lambda at, there: images[:, there], own)
                own_ref.wait()
                energy(slot)
                energy(pair_slot)
    bg_k.wait_recv()
    bg_d = remote(bg.at[other], bg.at[other], bsend.at[np_ + 2], brecv.at[np_ + 2], "img", cp)
    bg_d.start()

    fwd = []

    def forward_img(i):
        arrive(img_k[i])
        fwd.append(send_img(pair_img.at[chunk(i)], img_all.at[other, chunk(i)], cp))
        normalise(lambda at, there: pair_img[chunk(i), at], other, chunk(i))

    forward_img(0)
    bg_c.wait_recv()
    for x in img_across:
        arrive(x)
    normalise(lambda at, there: img_all[across, :, at], across)
    forward_img(1)
    for j, (b, w) in enumerate(order):
        for x, s in stage[j]:
            arrive(x)
            energy(s + w * (1 - 2 * bit(d, b)))
    erow[...] = jnp.transpose(ecol[...].reshape(-1, 128))[0:8]

    nv = nviews * n // 2
    kt = min(1024, q)

    def score(s):
        partial[s] = jnp.broadcast_to(-0.5 * erow[0:1, :], (rows, nv))

        def tile(t, _):
            at = aligned(t * kt, kt, 128)
            partial[s] += lax.dot_general(
                img_all[s, :, at], ref_all[:, :, at].reshape(nv, kt),
                (((1,), (1,)), ((), ())), preferred_element_type=F32)
            return 0
        lax.fori_loop(0, q // kt, tile, 0)

    cuts = [("pix", b, flip(p, b), bit(p, b)) for b in pbits] + [("img", PIXEL_BIT, kp, k)]
    nc = len(cuts)
    starts, sizes = [0], [rows]
    for axis, b, partner, mybit in cuts:
        sizes.append(sizes[-1] // 2)
        starts.append(starts[-1] + mybit * sizes[-1])

    def halve(j, s):
        axis, b, partner, mybit = cuts[j]
        gone = aligned(starts[j] + (1 - mybit) * sizes[j + 1], sizes[j + 1], sizes[j + 1])
        return remote(partial.at[s, gone], halves[j].at[s], hsend.at[j, s], hrecv.at[j, s], axis, partner)

    def absorb_half(j, s):
        halve(j, s).wait_recv()
        held = aligned(starts[j + 1], sizes[j + 1], sizes[j + 1])
        partial[s, held, :] += halves[j][s]

    def begin(s):
        score(s)
        halve(0, s).start()

    def middle(*slots):
        for j in range(nc - 1):
            for s in slots:
                absorb_half(j, s)
                halve(j + 1, s).start()

    nlast = sizes[-1]
    held = aligned(starts[-1], nlast, nlast)
    lane2 = lax.broadcasted_iota(jnp.int32, (nlast, 128), 1)

    def soft_copy(s):
        return remote(soft.at[s], soft_in.at[s], csend.at[s], crecv.at[s], "img", cp)

    def soften(s):
        absorb_half(nc - 1, s)
        x = partial[s, held, :] * (4.0 / SIDE)
        partial[s, held, :] = x
        top = jnp.max(x, 1, keepdims=True)
        soft[s] = jnp.where(
            lane2 == 0, top,
            jnp.where(lane2 == 1, jnp.sum(jnp.exp(x - top), 1, keepdims=True),
                      jnp.sum(x, 1, keepdims=True)))
        soft_copy(s).start()

    def grow(j, s):
        axis, b, partner, mybit = cuts[j]
        at = aligned(starts[j + 1], sizes[j + 1], sizes[j + 1])
        return remote(post.at[s, at], post.at[s, at], gsend.at[j, s], grecv.at[j, s], axis, partner)

    def settle(s):
        soft_copy(s).wait_recv()
        a, b = soft[s], soft_in[s]
        top = jnp.maximum(a[:, 0:1], b[:, 0:1])
        exps = a[:, 1:2] * jnp.exp(a[:, 0:1] - top) + b[:, 1:2] * jnp.exp(b[:, 0:1] - top)
        log_total = top + jnp.log(exps)
        evb[s] = jnp.broadcast_to(
            log_total - (a[:, 2:3] + b[:, 2:3]) / (nviews * n), (nlast, 128))
        post[s, held, :] = jnp.exp(partial[s, held, :] - log_total).astype(BF16)
        grow(nc - 1, s).start()

    begin(own)
    begin(across)
    for i in range(2, CHUNKS - 1):
        forward_img(i)
    middle(own, across)
    forward_img(CHUNKS - 1)
    begin(other)
    bg_d.wait_recv()

    def take_diag(i):
        arrive(fwd[i])
        normalise(lambda at, there: img_all[diag, chunk(i), at], diag, chunk(i))

    for i in range(CHUNKS - 1):
        take_diag(i)
    middle(other)
    take_diag(CHUNKS - 1)
    begin(diag)
    soften(other)
    soften(own)
    middle(diag)
    soften(diag)
    soften(across)
    turns = [diag, across, other, own]
    for s in turns:
        settle(s)
    for j in range(nc - 1, 0, -1):
        for s in turns:
            grow(j, s).wait_recv()
            grow(j - 1, s).start()

    half0 = nv // 2
    class_mass = jnp.zeros((1, nv), F32)
    for s in turns:
        grow(0, s).wait_recv()
        x = post[s].astype(F32)
        xt = jnp.transpose(x).astype(BF16)
        at = aligned(s * rows, rows, 128)
        post_t[0, :, at] = xt[:half0]
        post_t[1, :, at] = xt[half0:]
        class_mass = class_mass + jnp.sum(x, 0, keepdims=True)

    tiles = pixel_tiles(q)
    wt = q // tiles
    partners = [flip(d, b) for b in bits]
    mybits = [bit(d, b) for b in bits] + [k]

    def tile_cols(t):
        return aligned(t * wt, wt, 128)

    def weigh(half, t):
        return jnp.dot(post_t[half], img_all[:, :, tile_cols(t)].reshape(4 * rows, wt),
                       preferred_element_type=F32)

    def stage_copy(j, t):
        return remote(sends[j].at[t], recvs[j].at[t], vsend.at[j, t], vrecv.at[j, t],
                      "img", partners[j])

    def last_copy(t):
        place = aligned(k * q + t * wt, wt, 128)
        return remote(last.at[t], out.at[:, place], vsend.at[nr, t], vrecv.at[nr, t], "img", kp)

    def first(t, _):
        sends[0][t] = weigh(1 - mybits[0], t).astype(BF16)
        stage_copy(0, t).start()
        return 0

    lax.fori_loop(0, tiles, first, 0)

    ev_all[aligned(k * nlast, nlast, nlast), :] = evb[own]
    ev_copy = remote(evb.at[other], ev_all.at[aligned(k * nlast, nlast, nlast)],
                     esend.at[0], erecv.at[0], "img", kp)
    ev_copy.start()

    hit = lax.broadcasted_iota(jnp.int32, (NCLS, nv), 0) == classes[...]
    mass[0] = jnp.broadcast_to(
        jnp.sum(jnp.where(hit, class_mass, 0.0), 1, keepdims=True), (NCLS, 128))
    mass_hops = [*bits, VIEW_BIT]

    def mass_copy(j):
        return remote(mass.at[j], mass_in.at[j], ksend.at[j], krecv.at[j], "img", flip(d, mass_hops[j]))

    mass_copy(0).start()

    def mass_hop(j):
        if j < len(mass_hops):
            mass_copy(j).wait()
            mass[j + 1] = mass[j] + mass_in[j]
            if j + 1 < len(mass_hops):
                mass_copy(j + 1).start()

    def absorb(j, t):
        size = half0 >> (j + 1)
        there = aligned((1 - mybits[j + 1]) * size, size, 16)
        here = aligned(mybits[j + 1] * size, size, 16)
        if j == 0:
            fresh[...] = weigh(mybits[0], t)
            base = fresh
        else:
            base = keep[j - 1].at[t]
        stage_copy(j, t).wait_recv()
        gone = base[there, :] + recvs[j][t, there, :].astype(F32)
        if j + 1 < nr:
            sends[j + 1][t] = gone.astype(BF16)
            stage_copy(j + 1, t).start()
        else:
            last[t] = gone
            last_copy(t).start()
        rest = base[here, :] + recvs[j][t, here, :].astype(F32)
        if j + 1 < nr:
            keep[j][t] = rest
        else:
            out[:, aligned(k * q + t * wt, wt, 128)] = rest

    def steps(t):
        for j in range(nr):
            absorb(j, t - j)

    def ramp(ts):
        for t in ts:
            for j in range(nr):
                if 0 <= t - j < tiles:
                    absorb(j, t - j)

    ramp(range(nr - 1))
    mass_hop(0)
    lax.fori_loop(nr - 1, tiles // 2, lambda t, _: (steps(t), 0)[1], 0)
    mass_hop(1)
    lax.fori_loop(tiles // 2, tiles, lambda t, _: (steps(t), 0)[1], 0)
    for j in range(2, len(mass_hops)):
        mass_hop(j)
    cls_out[...] = jnp.transpose(mass[len(mass_hops)] * (NCLS / total))[0:1]
    ramp(range(tiles, tiles + nr - 1))

    for x in ref_copies + img_copies + [bg_k, bg_c, bg_d]:
        x.wait_send()
    ev_copy.wait()
    ev_out[...] = jnp.transpose(ev_all[...])[0:1]

    def drain(s, _):
        soft_copy(s).wait_send()
        for j in range(nc):
            halve(j, s).wait_send()
            grow(j, s).wait_send()
        return 0

    lax.fori_loop(0, 4, drain, 0)

    def finish(t, _):
        last_copy(t).wait()
        for j in range(nr):
            stage_copy(j, t).wait_send()
        return 0

    lax.fori_loop(0, tiles, finish, 0)


def whole_step(n, m, images, refs, mask, classes):
    rows, cols = images.shape
    nviews = refs.shape[0]
    q = cols // 2
    bits = image_bits(n)
    nr = len(bits)
    nb = nr + 2
    npix = len(low_bits(m))
    nc = npix + 1
    nv = nviews * n // 2
    half0 = nv // 2
    tiles = pixel_tiles(q)
    wt = q // tiles
    nlast = rows >> nc
    n_ref = 1 + sum(2 ** (j + 1) for j in range(nr))
    n_img = 3 * CHUNKS
    vm = pl.BlockSpec(memory_space=pltpu.VMEM)
    hbm = pl.BlockSpec(memory_space=pl.ANY)
    V = pltpu.VMEM
    dma = pltpu.SemaphoreType.DMA
    scratch = [
        V((4, rows, q), BF16), V((rows, q), BF16), V((n // 2, nviews, q), BF16),
        V((nb + 1, 2, cols), F32), V((nb, 2, cols), F32), V((2, cols), F32),
        V((4, rows, 128), F32), V((npix + 1, rows, 128), F32), V((npix, rows, 128), F32),
        V((n // 2, nviews, 128), F32), V((8, nv), F32),
        V((4, rows, nv), F32), [V((4, rows >> (j + 1), nv), F32) for j in range(nc)],
        V((4, nlast, 128), F32), V((4, nlast, 128), F32), V((4, nlast, 128), F32),
        V((rows // m, 128), F32),
        V((4, rows, nv), BF16), V((2, half0, 4 * rows), BF16),
        V((nb, NCLS, 128), F32), V((nb - 1, NCLS, 128), F32),
        V((half0, wt), F32),
        [V((tiles, half0 >> (j + 1), wt), F32) for j in range(nr - 1)],
        [V((tiles, half0 >> j, wt), BF16) for j in range(nr)],
        [V((tiles, half0 >> j, wt), BF16) for j in range(nr)],
        V((tiles, nviews, wt), F32),
        dma((1,)), dma((n_img,)), dma((n_img,)), dma((n_ref,)), dma((n_ref,)),
        dma((nb,)), dma((nb,)), dma((npix + 3,)), dma((npix + 3,)),
        dma((nc, 4)), dma((nc, 4)), dma((4,)), dma((4,)), dma((nc, 4)), dma((nc, 4)),
        dma((nr + 1, tiles)), dma((nr + 1, tiles)), dma((nb - 1,)), dma((nb - 1,)),
        dma((1,)), dma((1,)),
    ]
    return pl.pallas_call(
        functools.partial(kernel, n, m),
        out_shape=(
            jax.ShapeDtypeStruct((nviews, cols), F32),
            jax.ShapeDtypeStruct((1, rows // m), F32),
            jax.ShapeDtypeStruct((1, NCLS), F32),
        ),
        in_specs=[vm, hbm, vm, vm],
        out_specs=(vm, vm, vm),
        scratch_shapes=scratch,
        compiler_params=pltpu.CompilerParams(
            collective_id=0, has_side_effects=True, vmem_limit_bytes=62 * 2**20),
    )(images, refs, mask, classes)


def on_device(images, references, cycle_mask, view_class):
    n = lax.axis_size("img")
    m = lax.axis_size("pix")
    c = bit(lax.axis_index("img"), VIEW_BIT)
    nviews = references.shape[0]
    bits = image_bits(n)
    nr = len(bits)
    owner = []
    for slot in range(n // 2):
        at = (slot % 2) * PIXEL_BIT
        for j, b in enumerate(bits):
            at = at + ((slot // 2 ** (nr - j)) % 2) * b
        owner.append(at)
    by_owner = view_class.reshape(n, nviews)
    groups = [
        jnp.concatenate([by_owner[at + g * VIEW_BIT] for at in owner]) for g in range(2)
    ]
    classes = jnp.where(c == 0, groups[0], groups[1])[None, :]
    view_sums, evidence, class_share = whole_step(
        n, m, images, references, cycle_mask[None, :], classes)
    return (view_sums, class_share[0], evidence[0])


def solution(mesh):
    in_specs = (P("img", "pix"), P("img", "pix"), P("pix"), P())
    out_specs = (P("img", "pix"), P(), P(("img", "pix")))
    return jax.shard_map(
        on_device, mesh=mesh, in_specs=in_specs, out_specs=out_specs, check_vma=False
    )
```

```python
import functools

import jax
import jax.numpy as jnp
from jax import lax
from jax.experimental import pallas as pl
from jax.experimental.pallas import tpu as pltpu
from jax.sharding import PartitionSpec as P

SIDE = 128
NCLS = 96
EPSILON = 1e-05
MESH = pl.DeviceIdType.MESH
F32 = jnp.float32
BF16 = jnp.bfloat16

PIXEL_BIT = 4
VIEW_BIT = 2
CHUNKS = 4


def image_bits(n):
    return [b for b in (1, *reversed([2**j for j in range(3, 20) if 2**j < n]))]


def low_bits(m):
    return [2**j for j in range(20) if 2**j < m]


def pixel_tiles(q):
    return min(16, q // 128)


def bit(index, value):
    return (index // value) % 2


def flip(index, value):
    return index + value * (1 - 2 * bit(index, value))


def aligned(start, size, unit):
    return pl.ds(pl.multiple_of(start, unit), size)


def kernel(n, m, images, refs, mask, classes, out, ev_out, cls_out,
           img_all, pair_img, ref_all, stat, stat_in, col, bg, bg_mine, bg_in,
           ecol, erow, partial, halves, soft, soft_in, evb, ev_all, post, post_t,
           mass, mass_in, fresh, keep, sends, recvs, last,
           lsem, isend, irecv, rsend, rrecv, tsend, trecv, bsend, brecv,
           hsend, hrecv, csend, crecv, gsend, grecv, vsend, vrecv, ksend, krecv,
           esend, erecv):
    d = lax.axis_index("img")
    p = lax.axis_index("pix")
    bits = image_bits(n)
    nr = len(bits)
    pbits = list(reversed(low_bits(m)))
    k, c = bit(d, PIXEL_BIT), bit(d, VIEW_BIT)
    kp, cp = flip(d, PIXEL_BIT), flip(d, VIEW_BIT)
    rows, cols = images.shape
    nviews = refs.shape[0]
    q = cols // 2
    mine = aligned(k * q, q, 128)
    theirs = aligned((1 - k) * q, q, 128)
    weights = [2 ** (nr - j) for j in range(nr)]
    slot = k
    for b, w in zip(bits, weights):
        slot = slot + w * bit(d, b)
    own = 2 * c + k
    other = 2 * c + 1 - k
    across = 2 * (1 - c) + k
    diag = 2 * (1 - c) + 1 - k

    barrier = pltpu.get_barrier_semaphore()
    img_partners = [kp, cp] + [flip(d, b) for b in bits]
    for x in img_partners:
        pl.semaphore_signal(barrier, inc=1, device_id={"img": x}, device_id_type=MESH)
    for b in pbits:
        pl.semaphore_signal(barrier, inc=1, device_id={"pix": flip(p, b)}, device_id_type=MESH)
    pl.semaphore_wait(barrier, len(img_partners) + len(pbits))

    def remote(src, dst, ssem, rsem, axis, partner):
        return pltpu.make_async_remote_copy(
            src_ref=src, dst_ref=dst, send_sem=ssem, recv_sem=rsem,
            device_id={axis: partner}, device_id_type=MESH)

    ref_copies = []
    img_copies = []
    waited = []

    def send_ref(src, s, partner):
        i = len(ref_copies)
        x = remote(src, ref_all.at[s], rsend.at[i], rrecv.at[i], "img", partner)
        x.start()
        ref_copies.append(x)
        return x

    def send_img(src, dst, partner):
        i = len(img_copies)
        x = remote(src, dst, isend.at[i], irecv.at[i], "img", partner)
        x.start()
        img_copies.append(x)
        return x

    def arrive(x):
        if all(x is not y for y in waited):
            x.wait_recv()
            waited.append(x)

    step = rows // CHUNKS

    def chunk(i):
        return pl.ds(i * step, step)

    order = list(reversed(list(zip(bits, weights))))
    stage = [[] for _ in order]

    def spread(src, s, first, stop):
        for j in range(first, stop):
            stage[j].append((send_ref(src, s, flip(d, order[j][0])), s))

    far = len(order) - 1
    spread(refs.at[:, mine], slot, far, far + 1)
    img_across = []

    def send_across(i):
        img_across.append(send_img(images.at[chunk(i), mine], img_all.at[own, chunk(i)], cp))

    img_k = []

    def send_pair(i):
        img_k.append(send_img(images.at[chunk(i), theirs], pair_img.at[chunk(i)], kp))

    send_across(0)
    send_pair(0)
    own_ref = pltpu.make_async_copy(refs.at[:, mine], ref_all.at[slot], lsem.at[0])
    own_ref.start()

    wide = min(512, cols)

    def col_tile(t, _):
        at = aligned(t * wide, wide, 128)
        x = images[:, at].astype(F32)
        stat[0, 0:1, at] = jnp.sum(x, 0, keepdims=True)
        stat[0, 1:2, at] = jnp.sum(x * x, 0, keepdims=True)
        return 0

    lax.fori_loop(0, cols // wide, col_tile, 0)
    hops = [PIXEL_BIT, *[b for b, _ in order[:-1]], VIEW_BIT, order[-1][0]]

    def hop(j):
        x = remote(stat.at[j], stat_in.at[j], tsend.at[j], trecv.at[j], "img", flip(d, hops[j]))
        x.start()
        x.wait()
        stat[j + 1] = stat[j] + stat_in[j]

    for j in range(len(order)):
        hop(j)
    pair_ref = send_ref(refs.at[:, theirs], slot, kp)
    spread(refs.at[:, mine], slot, 0, far)
    hop(len(order))
    send_across(1)
    hop(len(order) + 1)
    total = rows * n
    nh = len(hops)
    col_mean = stat[nh, 0:1, :] / total
    col[0:1, :] = col_mean
    col[1:2, :] = 1.0 / jnp.sqrt(stat[nh, 1:2, :] / total - col_mean * col_mean + EPSILON)

    def bg_tile(t, carry):
        s, sq, cnt = carry
        at = aligned(t * wide, wide, 128)
        w = (images[:, at].astype(F32) - col[0:1, at]) * col[1:2, at]
        mk = mask[:, at].astype(F32)
        wm = w * mk
        wq = wm * w
        for i in range(wide // 128):
            part = slice(i * 128, (i + 1) * 128)
            s = s + wm[:, part]
            sq = sq + wq[:, part]
            cnt = cnt + mk[:, part]
        return s, sq, cnt

    zero = jnp.zeros((rows, 128), F32)
    s, sq, cnt = lax.fori_loop(0, cols // wide, bg_tile, (zero, zero, jnp.zeros((1, 128), F32)))
    lane = lax.broadcasted_iota(jnp.int32, (rows, 128), 1)
    bg_mine[0] = jnp.where(
        lane == 0, jnp.sum(s, 1, keepdims=True),
        jnp.where(lane == 1, jnp.sum(sq, 1, keepdims=True), jnp.sum(cnt, 1, keepdims=True)))
    for j, b in enumerate(pbits):
        x = remote(bg_mine.at[j], bg_in.at[j], bsend.at[j], brecv.at[j], "pix", flip(p, b))
        x.start()
        x.wait()
        bg_mine[j + 1] = bg_mine[j] + bg_in[j]
    np_ = len(pbits)
    sums = bg_mine[np_]
    count = sums[:, 2:3]
    bg_mean = sums[:, 0:1] / count
    bg_inv = 1.0 / jnp.sqrt(sums[:, 1:2] / count - bg_mean * bg_mean + EPSILON)
    bg[own] = jnp.where(lane == 0, bg_mean, bg_inv)
    bg_k = remote(bg.at[own], bg.at[own], bsend.at[np_], brecv.at[np_], "img", kp)
    bg_k.start()
    bg_c = remote(bg.at[own], bg.at[own], bsend.at[np_ + 1], brecv.at[np_ + 1], "img", cp)
    bg_c.start()

    ncol = min(512, q)

    def normalise(read, s, r=pl.ds(0, rows)):
        def tile(t, _):
            at = aligned(t * ncol, ncol, 128)
            there = aligned(k * q + t * ncol, ncol, 128)
            w = (read(at, there).astype(F32) - col[0:1, there]) * col[1:2, there]
            img_all[s, r, at] = ((w - bg[s, r, 0:1]) * bg[s, r, 1:2]).astype(BF16)
            return 0
        lax.fori_loop(0, q // ncol, tile, 0)

    def energy(s):
        def tile(t, acc):
            x = ref_all[s, :, aligned(t * ncol, ncol, 128)].astype(F32)
            x = x * x
            for i in range(ncol // 128):
                acc = acc + x[:, i * 128:(i + 1) * 128]
            return acc
        acc = lax.fori_loop(0, q // ncol, tile, jnp.zeros((nviews, 128), F32))
        ecol[s] = jnp.broadcast_to(jnp.sum(acc, 1, keepdims=True), (nviews, 128))

    fwd = []

    def forward_img(i):
        arrive(img_k[i])
        fwd.append(send_img(pair_img.at[chunk(i)], img_all.at[other, chunk(i)], cp))

    def take_pair(i):
        normalise(lambda at, there: pair_img[chunk(i), at], other, chunk(i))

    for i in range(2, CHUNKS):
        send_across(i)
    forward_img(0)
    arrive(pair_ref)
    pair_slot = slot + 1 - 2 * k
    spread(ref_all.at[pair_slot], pair_slot, 0, far)
    for i in range(1, CHUNKS):
        send_pair(i)
    spread(ref_all.at[pair_slot], pair_slot, far, far + 1)
    normalise(lambda at, there: images[:, there], own)
    own_ref.wait()
    energy(slot)
    energy(pair_slot)
    bg_k.wait_recv()
    bg_d = remote(bg.at[other], bg.at[other], bsend.at[np_ + 2], brecv.at[np_ + 2], "img", cp)
    bg_d.start()
    ready = 0
    for j, (b, w) in enumerate(order[:-1]):
        for x, s in stage[j]:
            arrive(x)
            got = s + w * (1 - 2 * bit(d, b))
            spread(ref_all.at[got], got, j + 1, len(order))
            energy(got)
            if ready == 0:
                take_pair(0)
                bg_c.wait_recv()
                for y in img_across:
                    arrive(y)
                normalise(lambda at, there: img_all[across, :, at], across)
            ready += 1
    forward_img(1)
    take_pair(1)
    for x, s in stage[far]:
        arrive(x)
        energy(s + order[far][1] * (1 - 2 * bit(d, order[far][0])))
    erow[...] = jnp.transpose(ecol[...].reshape(-1, 128))[0:8]

    nv = nviews * n // 2
    kt = min(1024, q)

    def score(s):
        partial[s] = jnp.broadcast_to(-0.5 * erow[0:1, :], (rows, nv))

        def tile(t, _):
            at = aligned(t * kt, kt, 128)
            partial[s] += lax.dot_general(
                img_all[s, :, at], ref_all[:, :, at].reshape(nv, kt),
                (((1,), (1,)), ((), ())), preferred_element_type=F32)
            return 0
        lax.fori_loop(0, q // kt, tile, 0)

    cuts = [("pix", b, flip(p, b), bit(p, b)) for b in pbits] + [("img", PIXEL_BIT, kp, k)]
    nc = len(cuts)
    starts, sizes = [0], [rows]
    for axis, b, partner, mybit in cuts:
        sizes.append(sizes[-1] // 2)
        starts.append(starts[-1] + mybit * sizes[-1])

    def halve(j, s):
        axis, b, partner, mybit = cuts[j]
        gone = aligned(starts[j] + (1 - mybit) * sizes[j + 1], sizes[j + 1], sizes[j + 1])
        return remote(partial.at[s, gone], halves[j].at[s], hsend.at[j, s], hrecv.at[j, s], axis, partner)

    def absorb_half(j, s):
        halve(j, s).wait_recv()
        held = aligned(starts[j + 1], sizes[j + 1], sizes[j + 1])
        partial[s, held, :] += halves[j][s]

    def begin(s):
        score(s)
        halve(0, s).start()

    def middle(*slots):
        for j in range(nc - 1):
            for s in slots:
                absorb_half(j, s)
                halve(j + 1, s).start()

    nlast = sizes[-1]
    held = aligned(starts[-1], nlast, nlast)
    lane2 = lax.broadcasted_iota(jnp.int32, (nlast, 128), 1)

    def soft_copy(s):
        return remote(soft.at[s], soft_in.at[s], csend.at[s], crecv.at[s], "img", cp)

    def soften(s):
        absorb_half(nc - 1, s)
        x = partial[s, held, :] * (4.0 / SIDE)
        partial[s, held, :] = x
        top = jnp.max(x, 1, keepdims=True)
        soft[s] = jnp.where(
            lane2 == 0, top,
            jnp.where(lane2 == 1, jnp.sum(jnp.exp(x - top), 1, keepdims=True),
                      jnp.sum(x, 1, keepdims=True)))
        soft_copy(s).start()

    def grow(j, s):
        axis, b, partner, mybit = cuts[j]
        at = aligned(starts[j + 1], sizes[j + 1], sizes[j + 1])
        return remote(post.at[s, at], post.at[s, at], gsend.at[j, s], grecv.at[j, s], axis, partner)

    def settle(s):
        soft_copy(s).wait_recv()
        a, b = soft[s], soft_in[s]
        top = jnp.maximum(a[:, 0:1], b[:, 0:1])
        exps = a[:, 1:2] * jnp.exp(a[:, 0:1] - top) + b[:, 1:2] * jnp.exp(b[:, 0:1] - top)
        log_total = top + jnp.log(exps)
        evb[s] = jnp.broadcast_to(
            log_total - (a[:, 2:3] + b[:, 2:3]) / (nviews * n), (nlast, 128))
        post[s, held, :] = jnp.exp(partial[s, held, :] - log_total).astype(BF16)
        grow(nc - 1, s).start()

    for i in range(2, CHUNKS - 1):
        forward_img(i)
        take_pair(i)
    begin(own)
    begin(across)
    forward_img(CHUNKS - 1)
    take_pair(CHUNKS - 1)
    middle(own, across)
    begin(other)
    bg_d.wait_recv()

    def take_diag(i):
        arrive(fwd[i])
        normalise(lambda at, there: img_all[diag, chunk(i), at], diag, chunk(i))

    for i in range(CHUNKS - 1):
        take_diag(i)
    middle(other)
    take_diag(CHUNKS - 1)
    begin(diag)
    soften(other)
    soften(own)
    middle(diag)
    soften(diag)
    soften(across)
    turns = [diag, across, other, own]
    for s in turns:
        settle(s)
    for j in range(nc - 1, 0, -1):
        for s in turns:
            grow(j, s).wait_recv()
            grow(j - 1, s).start()

    half0 = nv // 2
    class_mass = jnp.zeros((1, nv), F32)
    for s in turns:
        grow(0, s).wait_recv()
        x = post[s].astype(F32)
        xt = jnp.transpose(x).astype(BF16)
        at = aligned(s * rows, rows, 128)
        post_t[0, :, at] = xt[:half0]
        post_t[1, :, at] = xt[half0:]
        class_mass = class_mass + jnp.sum(x, 0, keepdims=True)

    tiles = pixel_tiles(q)
    wt = q // tiles
    partners = [flip(d, b) for b in bits]
    mybits = [bit(d, b) for b in bits] + [k]

    def tile_cols(t):
        return aligned(t * wt, wt, 128)

    def weigh(half, t):
        return jnp.dot(post_t[half], img_all[:, :, tile_cols(t)].reshape(4 * rows, wt),
                       preferred_element_type=F32)

    def stage_copy(j, t):
        return remote(sends[j].at[t], recvs[j].at[t], vsend.at[j, t], vrecv.at[j, t],
                      "img", partners[j])

    def last_copy(t):
        place = aligned(k * q + t * wt, wt, 128)
        return remote(last.at[t], out.at[:, place], vsend.at[nr, t], vrecv.at[nr, t], "img", kp)

    hit = lax.broadcasted_iota(jnp.int32, (NCLS, nv), 0) == classes[...]
    mass[0] = jnp.broadcast_to(
        jnp.sum(jnp.where(hit, class_mass, 0.0), 1, keepdims=True), (NCLS, 128))
    mass_hops = [*bits, VIEW_BIT]

    def mass_copy(j):
        return remote(mass.at[j], mass_in.at[j], ksend.at[j], krecv.at[j], "img", flip(d, mass_hops[j]))

    def mass_hop(j):
        mass_copy(j).wait()
        mass[j + 1] = mass[j] + mass_in[j]
        if j + 1 < len(mass_hops):
            mass_copy(j + 1).start()

    mass_copy(0).start()

    ev_all[aligned(k * nlast, nlast, nlast), :] = evb[own]
    ev_copy = remote(evb.at[other], ev_all.at[aligned(k * nlast, nlast, nlast)],
                     esend.at[0], erecv.at[0], "img", kp)
    ev_copy.start()

    def first(t, _):
        sends[0][t] = weigh(1 - mybits[0], t).astype(BF16)
        stage_copy(0, t).start()
        return 0

    lax.fori_loop(0, tiles, first, 0)
    mass_hop(0)

    def absorb(j, t):
        size = half0 >> (j + 1)
        there = aligned((1 - mybits[j + 1]) * size, size, 16)
        here = aligned(mybits[j + 1] * size, size, 16)
        if j == 0:
            fresh[...] = weigh(mybits[0], t)
            base = fresh
        else:
            base = keep[j - 1].at[t]
        stage_copy(j, t).wait_recv()
        gone = base[there, :] + recvs[j][t, there, :].astype(F32)
        if j + 1 < nr:
            sends[j + 1][t] = gone.astype(BF16)
            stage_copy(j + 1, t).start()
        else:
            last[t] = gone
            last_copy(t).start()
        rest = base[here, :] + recvs[j][t, here, :].astype(F32)
        if j + 1 < nr:
            keep[j][t] = rest
        else:
            out[:, aligned(k * q + t * wt, wt, 128)] = rest

    def steps(t):
        for j in range(nr):
            absorb(j, t - j)

    def ramp(ts):
        for t in ts:
            for j in range(nr):
                if 0 <= t - j < tiles:
                    absorb(j, t - j)

    ramp(range(nr - 1))
    lax.fori_loop(nr - 1, tiles, lambda t, _: (steps(t), 0)[1], 0)
    mass_hop(1)
    ramp(range(tiles, tiles + nr - 1))
    for j in range(2, len(mass_hops)):
        mass_hop(j)
    cls_out[...] = jnp.transpose(mass[len(mass_hops)] * (NCLS / total))[0:1]

    for x in ref_copies + img_copies + [bg_k, bg_c, bg_d]:
        x.wait_send()
    ev_copy.wait()
    ev_out[...] = jnp.transpose(ev_all[...])[0:1]

    def drain(s, _):
        soft_copy(s).wait_send()
        for j in range(nc):
            halve(j, s).wait_send()
            grow(j, s).wait_send()
        return 0

    lax.fori_loop(0, 4, drain, 0)

    def finish(t, _):
        last_copy(t).wait()
        for j in range(nr):
            stage_copy(j, t).wait_send()
        return 0

    lax.fori_loop(0, tiles, finish, 0)


def whole_step(n, m, images, refs, mask, classes):
    rows, cols = images.shape
    nviews = refs.shape[0]
    q = cols // 2
    bits = image_bits(n)
    nr = len(bits)
    nb = nr + 2
    npix = len(low_bits(m))
    nc = npix + 1
    nv = nviews * n // 2
    half0 = nv // 2
    tiles = pixel_tiles(q)
    wt = q // tiles
    nlast = rows >> nc
    n_ref = 1 + sum(2 ** (j + 1) for j in range(nr))
    n_img = 3 * CHUNKS
    vm = pl.BlockSpec(memory_space=pltpu.VMEM)
    hbm = pl.BlockSpec(memory_space=pl.ANY)
    V = pltpu.VMEM
    dma = pltpu.SemaphoreType.DMA
    scratch = [
        V((4, rows, q), BF16), V((rows, q), BF16), V((n // 2, nviews, q), BF16),
        V((nb + 1, 2, cols), F32), V((nb, 2, cols), F32), V((2, cols), F32),
        V((4, rows, 128), F32), V((npix + 1, rows, 128), F32), V((npix, rows, 128), F32),
        V((n // 2, nviews, 128), F32), V((8, nv), F32),
        V((4, rows, nv), F32), [V((4, rows >> (j + 1), nv), F32) for j in range(nc)],
        V((4, nlast, 128), F32), V((4, nlast, 128), F32), V((4, nlast, 128), F32),
        V((rows // m, 128), F32),
        V((4, rows, nv), BF16), V((2, half0, 4 * rows), BF16),
        V((nb, NCLS, 128), F32), V((nb - 1, NCLS, 128), F32),
        V((half0, wt), F32),
        [V((tiles, half0 >> (j + 1), wt), F32) for j in range(nr - 1)],
        [V((tiles, half0 >> j, wt), BF16) for j in range(nr)],
        [V((tiles, half0 >> j, wt), BF16) for j in range(nr)],
        V((tiles, nviews, wt), F32),
        dma((1,)), dma((n_img,)), dma((n_img,)), dma((n_ref,)), dma((n_ref,)),
        dma((nb,)), dma((nb,)), dma((npix + 3,)), dma((npix + 3,)),
        dma((nc, 4)), dma((nc, 4)), dma((4,)), dma((4,)), dma((nc, 4)), dma((nc, 4)),
        dma((nr + 1, tiles)), dma((nr + 1, tiles)), dma((nb - 1,)), dma((nb - 1,)),
        dma((1,)), dma((1,)),
    ]
    return pl.pallas_call(
        functools.partial(kernel, n, m),
        out_shape=(
            jax.ShapeDtypeStruct((nviews, cols), F32),
            jax.ShapeDtypeStruct((1, rows // m), F32),
            jax.ShapeDtypeStruct((1, NCLS), F32),
        ),
        in_specs=[vm, hbm, vm, vm],
        out_specs=(vm, vm, vm),
        scratch_shapes=scratch,
        compiler_params=pltpu.CompilerParams(
            collective_id=0, has_side_effects=True, vmem_limit_bytes=62 * 2**20),
    )(images, refs, mask, classes)


def on_device(images, references, cycle_mask, view_class):
    n = lax.axis_size("img")
    m = lax.axis_size("pix")
    c = bit(lax.axis_index("img"), VIEW_BIT)
    nviews = references.shape[0]
    bits = image_bits(n)
    nr = len(bits)
    owner = []
    for slot in range(n // 2):
        at = (slot % 2) * PIXEL_BIT
        for j, b in enumerate(bits):
            at = at + ((slot // 2 ** (nr - j)) % 2) * b
        owner.append(at)
    by_owner = view_class.reshape(n, nviews)
    groups = [
        jnp.concatenate([by_owner[at + g * VIEW_BIT] for at in owner]) for g in range(2)
    ]
    classes = jnp.where(c == 0, groups[0], groups[1])[None, :]
    view_sums, evidence, class_share = whole_step(
        n, m, images, references, cycle_mask[None, :], classes)
    return (view_sums, class_share[0], evidence[0])


def solution(mesh):
    in_specs = (P("img", "pix"), P("img", "pix"), P("pix"), P())
    out_specs = (P("img", "pix"), P(), P(("img", "pix")))
    return jax.shard_map(
        on_device, mesh=mesh, in_specs=in_specs, out_specs=out_specs, check_vma=False
    )
```

```python
import functools

import jax
import jax.numpy as jnp
from jax import lax
from jax.experimental import pallas as pl
from jax.experimental.pallas import tpu as pltpu
from jax.sharding import PartitionSpec as P

SIDE = 128
NCLS = 96
EPSILON = 1e-05
MESH = pl.DeviceIdType.MESH
F32 = jnp.float32
BF16 = jnp.bfloat16

PIXEL_BIT = 4
VIEW_BIT = 2
CHUNKS = 8


def image_bits(n):
    return [b for b in (1, *reversed([2**j for j in range(3, 20) if 2**j < n]))]


def low_bits(m):
    return [2**j for j in range(20) if 2**j < m]


def pixel_tiles(q):
    return min(16, q // 128)


def bit(index, value):
    return (index // value) % 2


def flip(index, value):
    return index + value * (1 - 2 * bit(index, value))


def aligned(start, size, unit):
    return pl.ds(pl.multiple_of(start, unit), size)


def kernel(n, m, images, refs, mask, classes, out, ev_out, cls_out,
           img_all, pair_img, ref_all, stat, stat_in, col, bg, bg_mine, bg_in,
           ecol, erow, partial, halves, soft, soft_in, evb, ev_all, post, post_t,
           mass, mass_in, fresh, keep, sends, recvs, last,
           lsem, isend, irecv, rsend, rrecv, tsend, trecv, bsend, brecv,
           hsend, hrecv, csend, crecv, gsend, grecv, vsend, vrecv, ksend, krecv,
           esend, erecv):
    d = lax.axis_index("img")
    p = lax.axis_index("pix")
    bits = image_bits(n)
    nr = len(bits)
    pbits = list(reversed(low_bits(m)))
    k, c = bit(d, PIXEL_BIT), bit(d, VIEW_BIT)
    kp, cp = flip(d, PIXEL_BIT), flip(d, VIEW_BIT)
    rows, cols = images.shape
    nviews = refs.shape[0]
    q = cols // 2
    mine = aligned(k * q, q, 128)
    theirs = aligned((1 - k) * q, q, 128)
    weights = [2 ** (nr - j) for j in range(nr)]
    slot = k
    for b, w in zip(bits, weights):
        slot = slot + w * bit(d, b)
    own = 2 * c + k
    other = 2 * c + 1 - k
    across = 2 * (1 - c) + k
    diag = 2 * (1 - c) + 1 - k

    barrier = pltpu.get_barrier_semaphore()
    img_partners = [kp, cp] + [flip(d, b) for b in bits]
    for x in img_partners:
        pl.semaphore_signal(barrier, inc=1, device_id={"img": x}, device_id_type=MESH)
    for b in pbits:
        pl.semaphore_signal(barrier, inc=1, device_id={"pix": flip(p, b)}, device_id_type=MESH)
    pl.semaphore_wait(barrier, len(img_partners) + len(pbits))

    def remote(src, dst, ssem, rsem, axis, partner):
        return pltpu.make_async_remote_copy(
            src_ref=src, dst_ref=dst, send_sem=ssem, recv_sem=rsem,
            device_id={axis: partner}, device_id_type=MESH)

    ref_copies = []
    img_copies = []
    waited = []

    def send_ref(src, s, partner):
        i = len(ref_copies)
        x = remote(src, ref_all.at[s], rsend.at[i], rrecv.at[i], "img", partner)
        x.start()
        ref_copies.append(x)
        return x

    def send_img(src, dst, partner):
        i = len(img_copies)
        x = remote(src, dst, isend.at[i], irecv.at[i], "img", partner)
        x.start()
        img_copies.append(x)
        return x

    def arrive(x):
        if all(x is not y for y in waited):
            x.wait_recv()
            waited.append(x)

    step = rows // CHUNKS

    def chunk(i):
        return pl.ds(i * step, step)

    order = list(reversed(list(zip(bits, weights))))
    stage = [[] for _ in order]

    def spread(src, s, first, stop):
        for j in range(first, stop):
            stage[j].append((send_ref(src, s, flip(d, order[j][0])), s))

    far = len(order) - 1
    spread(refs.at[:, mine], slot, far, far + 1)
    img_across = []

    def send_across(i):
        img_across.append(send_img(images.at[chunk(i), mine], img_all.at[own, chunk(i)], cp))

    img_k = []

    def send_pair(i):
        img_k.append(send_img(images.at[chunk(i), theirs], pair_img.at[chunk(i)], kp))

    send_across(0)
    send_pair(0)
    own_ref = pltpu.make_async_copy(refs.at[:, mine], ref_all.at[slot], lsem.at[0])
    own_ref.start()

    wide = min(512, cols)

    def col_tile(t, _):
        at = aligned(t * wide, wide, 128)
        x = images[:, at].astype(F32)
        stat[0, 0:1, at] = jnp.sum(x, 0, keepdims=True)
        stat[0, 1:2, at] = jnp.sum(x * x, 0, keepdims=True)
        return 0

    lax.fori_loop(0, cols // wide, col_tile, 0)
    hops = [PIXEL_BIT, *[b for b, _ in order[:-1]], VIEW_BIT, order[-1][0]]

    def hop(j):
        x = remote(stat.at[j], stat_in.at[j], tsend.at[j], trecv.at[j], "img", flip(d, hops[j]))
        x.start()
        x.wait()
        stat[j + 1] = stat[j] + stat_in[j]

    for j in range(len(order)):
        hop(j)
    pair_ref = send_ref(refs.at[:, theirs], slot, kp)
    spread(refs.at[:, mine], slot, 0, far)
    hop(len(order))
    send_across(1)
    hop(len(order) + 1)
    total = rows * n
    nh = len(hops)
    col_mean = stat[nh, 0:1, :] / total
    col[0:1, :] = col_mean
    col[1:2, :] = 1.0 / jnp.sqrt(stat[nh, 1:2, :] / total - col_mean * col_mean + EPSILON)

    def bg_tile(t, carry):
        s, sq, cnt = carry
        at = aligned(t * wide, wide, 128)
        w = (images[:, at].astype(F32) - col[0:1, at]) * col[1:2, at]
        mk = mask[:, at].astype(F32)
        wm = w * mk
        wq = wm * w
        for i in range(wide // 128):
            part = slice(i * 128, (i + 1) * 128)
            s = s + wm[:, part]
            sq = sq + wq[:, part]
            cnt = cnt + mk[:, part]
        return s, sq, cnt

    zero = jnp.zeros((rows, 128), F32)
    s, sq, cnt = lax.fori_loop(0, cols // wide, bg_tile, (zero, zero, jnp.zeros((1, 128), F32)))
    lane = lax.broadcasted_iota(jnp.int32, (rows, 128), 1)
    bg_mine[0] = jnp.where(
        lane == 0, jnp.sum(s, 1, keepdims=True),
        jnp.where(lane == 1, jnp.sum(sq, 1, keepdims=True), jnp.sum(cnt, 1, keepdims=True)))
    for j, b in enumerate(pbits):
        x = remote(bg_mine.at[j], bg_in.at[j], bsend.at[j], brecv.at[j], "pix", flip(p, b))
        x.start()
        x.wait()
        bg_mine[j + 1] = bg_mine[j] + bg_in[j]
    np_ = len(pbits)
    sums = bg_mine[np_]
    count = sums[:, 2:3]
    bg_mean = sums[:, 0:1] / count
    bg_inv = 1.0 / jnp.sqrt(sums[:, 1:2] / count - bg_mean * bg_mean + EPSILON)
    bg[own] = jnp.where(lane == 0, bg_mean, bg_inv)
    bg_k = remote(bg.at[own], bg.at[own], bsend.at[np_], brecv.at[np_], "img", kp)
    bg_k.start()
    bg_c = remote(bg.at[own], bg.at[own], bsend.at[np_ + 1], brecv.at[np_ + 1], "img", cp)
    bg_c.start()

    ncol = min(512, q)

    def normalise(read, s, r=pl.ds(0, rows)):
        def tile(t, _):
            at = aligned(t * ncol, ncol, 128)
            there = aligned(k * q + t * ncol, ncol, 128)
            w = (read(at, there).astype(F32) - col[0:1, there]) * col[1:2, there]
            img_all[s, r, at] = ((w - bg[s, r, 0:1]) * bg[s, r, 1:2]).astype(BF16)
            return 0
        lax.fori_loop(0, q // ncol, tile, 0)

    def energy(s):
        def tile(t, acc):
            x = ref_all[s, :, aligned(t * ncol, ncol, 128)].astype(F32)
            x = x * x
            for i in range(ncol // 128):
                acc = acc + x[:, i * 128:(i + 1) * 128]
            return acc
        acc = lax.fori_loop(0, q // ncol, tile, jnp.zeros((nviews, 128), F32))
        ecol[s] = jnp.broadcast_to(jnp.sum(acc, 1, keepdims=True), (nviews, 128))

    fwd = []

    def forward_img(i):
        arrive(img_k[i])
        fwd.append(send_img(pair_img.at[chunk(i)], img_all.at[other, chunk(i)], cp))

    def take_pair(i):
        normalise(lambda at, there: pair_img[chunk(i), at], other, chunk(i))

    for i in range(2, CHUNKS):
        send_across(i)
    forward_img(0)
    arrive(pair_ref)
    pair_slot = slot + 1 - 2 * k
    spread(ref_all.at[pair_slot], pair_slot, 0, far)
    for i in range(1, CHUNKS):
        send_pair(i)
    spread(ref_all.at[pair_slot], pair_slot, far, far + 1)
    normalise(lambda at, there: images[:, there], own)
    own_ref.wait()
    energy(slot)
    energy(pair_slot)
    bg_k.wait_recv()
    bg_d = remote(bg.at[other], bg.at[other], bsend.at[np_ + 2], brecv.at[np_ + 2], "img", cp)
    bg_d.start()
    ready = 0
    for j, (b, w) in enumerate(order[:-1]):
        for x, s in stage[j]:
            arrive(x)
            got = s + w * (1 - 2 * bit(d, b))
            spread(ref_all.at[got], got, j + 1, len(order))
            energy(got)
            if ready == 0:
                take_pair(0)
                bg_c.wait_recv()
                for y in img_across:
                    arrive(y)
                normalise(lambda at, there: img_all[across, :, at], across)
            ready += 1
    forward_img(1)
    take_pair(1)
    for x, s in stage[far]:
        arrive(x)
        energy(s + order[far][1] * (1 - 2 * bit(d, order[far][0])))
    erow[...] = jnp.transpose(ecol[...].reshape(-1, 128))[0:8]

    nv = nviews * n // 2
    kt = min(1024, q)

    def score(s):
        partial[s] = jnp.broadcast_to(-0.5 * erow[0:1, :], (rows, nv))

        def tile(t, _):
            at = aligned(t * kt, kt, 128)
            partial[s] += lax.dot_general(
                img_all[s, :, at], ref_all[:, :, at].reshape(nv, kt),
                (((1,), (1,)), ((), ())), preferred_element_type=F32)
            return 0
        lax.fori_loop(0, q // kt, tile, 0)

    cuts = [("pix", b, flip(p, b), bit(p, b)) for b in pbits] + [("img", PIXEL_BIT, kp, k)]
    nc = len(cuts)
    starts, sizes = [0], [rows]
    for axis, b, partner, mybit in cuts:
        sizes.append(sizes[-1] // 2)
        starts.append(starts[-1] + mybit * sizes[-1])

    def halve(j, s):
        axis, b, partner, mybit = cuts[j]
        gone = aligned(starts[j] + (1 - mybit) * sizes[j + 1], sizes[j + 1], sizes[j + 1])
        return remote(partial.at[s, gone], halves[j].at[s], hsend.at[j, s], hrecv.at[j, s], axis, partner)

    def absorb_half(j, s):
        halve(j, s).wait_recv()
        held = aligned(starts[j + 1], sizes[j + 1], sizes[j + 1])
        partial[s, held, :] += halves[j][s]

    def begin(s):
        score(s)
        halve(0, s).start()

    def middle(*slots):
        for j in range(nc - 1):
            for s in slots:
                absorb_half(j, s)
                halve(j + 1, s).start()

    nlast = sizes[-1]
    held = aligned(starts[-1], nlast, nlast)
    lane2 = lax.broadcasted_iota(jnp.int32, (nlast, 128), 1)

    def soft_copy(s):
        return remote(soft.at[s], soft_in.at[s], csend.at[s], crecv.at[s], "img", cp)

    def soften(s):
        absorb_half(nc - 1, s)
        x = partial[s, held, :] * (4.0 / SIDE)
        partial[s, held, :] = x
        top = jnp.max(x, 1, keepdims=True)
        soft[s] = jnp.where(
            lane2 == 0, top,
            jnp.where(lane2 == 1, jnp.sum(jnp.exp(x - top), 1, keepdims=True),
                      jnp.sum(x, 1, keepdims=True)))
        soft_copy(s).start()

    def grow(j, s):
        axis, b, partner, mybit = cuts[j]
        at = aligned(starts[j + 1], sizes[j + 1], sizes[j + 1])
        return remote(post.at[s, at], post.at[s, at], gsend.at[j, s], grecv.at[j, s], axis, partner)

    def settle(s):
        soft_copy(s).wait_recv()
        a, b = soft[s], soft_in[s]
        top = jnp.maximum(a[:, 0:1], b[:, 0:1])
        exps = a[:, 1:2] * jnp.exp(a[:, 0:1] - top) + b[:, 1:2] * jnp.exp(b[:, 0:1] - top)
        log_total = top + jnp.log(exps)
        evb[s] = jnp.broadcast_to(
            log_total - (a[:, 2:3] + b[:, 2:3]) / (nviews * n), (nlast, 128))
        post[s, held, :] = jnp.exp(partial[s, held, :] - log_total).astype(BF16)
        grow(nc - 1, s).start()

    for i in range(2, CHUNKS - 1):
        forward_img(i)
        take_pair(i)
        if i == CHUNKS // 2:
            begin(own)
        if i == CHUNKS // 2 + 1:
            begin(across)
    forward_img(CHUNKS - 1)
    take_pair(CHUNKS - 1)
    middle(own, across)
    begin(other)
    bg_d.wait_recv()

    def take_diag(i):
        arrive(fwd[i])
        normalise(lambda at, there: img_all[diag, chunk(i), at], diag, chunk(i))

    for i in range(CHUNKS - 1):
        take_diag(i)
    middle(other)
    take_diag(CHUNKS - 1)
    begin(diag)
    soften(other)
    soften(own)
    middle(diag)
    soften(diag)
    soften(across)
    turns = [diag, across, other, own]
    for s in turns:
        settle(s)
    for j in range(nc - 1, 0, -1):
        for s in turns:
            grow(j, s).wait_recv()
            grow(j - 1, s).start()

    half0 = nv // 2
    class_mass = jnp.zeros((1, nv), F32)
    for s in turns:
        grow(0, s).wait_recv()
        x = post[s].astype(F32)
        xt = jnp.transpose(x).astype(BF16)
        at = aligned(s * rows, rows, 128)
        post_t[0, :, at] = xt[:half0]
        post_t[1, :, at] = xt[half0:]
        class_mass = class_mass + jnp.sum(x, 0, keepdims=True)

    tiles = pixel_tiles(q)
    wt = q // tiles
    partners = [flip(d, b) for b in bits]
    mybits = [bit(d, b) for b in bits] + [k]

    def tile_cols(t):
        return aligned(t * wt, wt, 128)

    def weigh(half, t):
        return jnp.dot(post_t[half], img_all[:, :, tile_cols(t)].reshape(4 * rows, wt),
                       preferred_element_type=F32)

    def stage_copy(j, t):
        return remote(sends[j].at[t], recvs[j].at[t], vsend.at[j, t], vrecv.at[j, t],
                      "img", partners[j])

    def last_copy(t):
        place = aligned(k * q + t * wt, wt, 128)
        return remote(last.at[t], out.at[:, place], vsend.at[nr, t], vrecv.at[nr, t], "img", kp)

    hit = lax.broadcasted_iota(jnp.int32, (NCLS, nv), 0) == classes[...]
    mass[0] = jnp.broadcast_to(
        jnp.sum(jnp.where(hit, class_mass, 0.0), 1, keepdims=True), (NCLS, 128))
    mass_hops = [*bits, VIEW_BIT]

    def mass_copy(j):
        return remote(mass.at[j], mass_in.at[j], ksend.at[j], krecv.at[j], "img", flip(d, mass_hops[j]))

    def mass_hop(j):
        mass_copy(j).wait()
        mass[j + 1] = mass[j] + mass_in[j]
        if j + 1 < len(mass_hops):
            mass_copy(j + 1).start()

    mass_copy(0).start()

    ev_all[aligned(k * nlast, nlast, nlast), :] = evb[own]
    ev_copy = remote(evb.at[other], ev_all.at[aligned(k * nlast, nlast, nlast)],
                     esend.at[0], erecv.at[0], "img", kp)
    ev_copy.start()

    def first(t, _):
        sends[0][t] = weigh(1 - mybits[0], t).astype(BF16)
        stage_copy(0, t).start()
        return 0

    lax.fori_loop(0, tiles, first, 0)
    mass_hop(0)

    def absorb(j, t):
        size = half0 >> (j + 1)
        there = aligned((1 - mybits[j + 1]) * size, size, 16)
        here = aligned(mybits[j + 1] * size, size, 16)
        if j == 0:
            fresh[...] = weigh(mybits[0], t)
            base = fresh
        else:
            base = keep[j - 1].at[t]
        stage_copy(j, t).wait_recv()
        gone = base[there, :] + recvs[j][t, there, :].astype(F32)
        if j + 1 < nr:
            sends[j + 1][t] = gone.astype(BF16)
            stage_copy(j + 1, t).start()
        else:
            last[t] = gone
            last_copy(t).start()
        rest = base[here, :] + recvs[j][t, here, :].astype(F32)
        if j + 1 < nr:
            keep[j][t] = rest
        else:
            out[:, aligned(k * q + t * wt, wt, 128)] = rest

    def steps(t):
        for j in range(nr):
            absorb(j, t - j)

    def ramp(ts):
        for t in ts:
            for j in range(nr):
                if 0 <= t - j < tiles:
                    absorb(j, t - j)

    ramp(range(nr - 1))
    lax.fori_loop(nr - 1, tiles, lambda t, _: (steps(t), 0)[1], 0)
    mass_hop(1)
    ramp(range(tiles, tiles + nr - 1))
    for j in range(2, len(mass_hops)):
        mass_hop(j)
    cls_out[...] = jnp.transpose(mass[len(mass_hops)] * (NCLS / total))[0:1]

    for x in ref_copies + img_copies + [bg_k, bg_c, bg_d]:
        x.wait_send()
    ev_copy.wait()
    ev_out[...] = jnp.transpose(ev_all[...])[0:1]

    def drain(s, _):
        soft_copy(s).wait_send()
        for j in range(nc):
            halve(j, s).wait_send()
            grow(j, s).wait_send()
        return 0

    lax.fori_loop(0, 4, drain, 0)

    def finish(t, _):
        last_copy(t).wait()
        for j in range(nr):
            stage_copy(j, t).wait_send()
        return 0

    lax.fori_loop(0, tiles, finish, 0)


def whole_step(n, m, images, refs, mask, classes):
    rows, cols = images.shape
    nviews = refs.shape[0]
    q = cols // 2
    bits = image_bits(n)
    nr = len(bits)
    nb = nr + 2
    npix = len(low_bits(m))
    nc = npix + 1
    nv = nviews * n // 2
    half0 = nv // 2
    tiles = pixel_tiles(q)
    wt = q // tiles
    nlast = rows >> nc
    n_ref = 1 + sum(2 ** (j + 1) for j in range(nr))
    n_img = 3 * CHUNKS
    vm = pl.BlockSpec(memory_space=pltpu.VMEM)
    hbm = pl.BlockSpec(memory_space=pl.ANY)
    V = pltpu.VMEM
    dma = pltpu.SemaphoreType.DMA
    scratch = [
        V((4, rows, q), BF16), V((rows, q), BF16), V((n // 2, nviews, q), BF16),
        V((nb + 1, 2, cols), F32), V((nb, 2, cols), F32), V((2, cols), F32),
        V((4, rows, 128), F32), V((npix + 1, rows, 128), F32), V((npix, rows, 128), F32),
        V((n // 2, nviews, 128), F32), V((8, nv), F32),
        V((4, rows, nv), F32), [V((4, rows >> (j + 1), nv), F32) for j in range(nc)],
        V((4, nlast, 128), F32), V((4, nlast, 128), F32), V((4, nlast, 128), F32),
        V((rows // m, 128), F32),
        V((4, rows, nv), BF16), V((2, half0, 4 * rows), BF16),
        V((nb, NCLS, 128), F32), V((nb - 1, NCLS, 128), F32),
        V((half0, wt), F32),
        [V((tiles, half0 >> (j + 1), wt), F32) for j in range(nr - 1)],
        [V((tiles, half0 >> j, wt), BF16) for j in range(nr)],
        [V((tiles, half0 >> j, wt), BF16) for j in range(nr)],
        V((tiles, nviews, wt), F32),
        dma((1,)), dma((n_img,)), dma((n_img,)), dma((n_ref,)), dma((n_ref,)),
        dma((nb,)), dma((nb,)), dma((npix + 3,)), dma((npix + 3,)),
        dma((nc, 4)), dma((nc, 4)), dma((4,)), dma((4,)), dma((nc, 4)), dma((nc, 4)),
        dma((nr + 1, tiles)), dma((nr + 1, tiles)), dma((nb - 1,)), dma((nb - 1,)),
        dma((1,)), dma((1,)),
    ]
    return pl.pallas_call(
        functools.partial(kernel, n, m),
        out_shape=(
            jax.ShapeDtypeStruct((nviews, cols), F32),
            jax.ShapeDtypeStruct((1, rows // m), F32),
            jax.ShapeDtypeStruct((1, NCLS), F32),
        ),
        in_specs=[vm, hbm, vm, vm],
        out_specs=(vm, vm, vm),
        scratch_shapes=scratch,
        compiler_params=pltpu.CompilerParams(
            collective_id=0, has_side_effects=True, vmem_limit_bytes=62 * 2**20),
    )(images, refs, mask, classes)


def on_device(images, references, cycle_mask, view_class):
    n = lax.axis_size("img")
    m = lax.axis_size("pix")
    c = bit(lax.axis_index("img"), VIEW_BIT)
    nviews = references.shape[0]
    bits = image_bits(n)
    nr = len(bits)
    owner = []
    for slot in range(n // 2):
        at = (slot % 2) * PIXEL_BIT
        for j, b in enumerate(bits):
            at = at + ((slot // 2 ** (nr - j)) % 2) * b
        owner.append(at)
    by_owner = view_class.reshape(n, nviews)
    groups = [
        jnp.concatenate([by_owner[at + g * VIEW_BIT] for at in owner]) for g in range(2)
    ]
    classes = jnp.where(c == 0, groups[0], groups[1])[None, :]
    view_sums, evidence, class_share = whole_step(
        n, m, images, references, cycle_mask[None, :], classes)
    return (view_sums, class_share[0], evidence[0])


def solution(mesh):
    in_specs = (P("img", "pix"), P("img", "pix"), P("pix"), P())
    out_specs = (P("img", "pix"), P(), P(("img", "pix")))
    return jax.shard_map(
        on_device, mesh=mesh, in_specs=in_specs, out_specs=out_specs, check_vma=False
    )
```
